256 devices in a mesh: row: 32 (over x, z_hi, core), col: 8 (over z_lo, y).
Axes of the slice: x: 4, y: 4, z: 8 (z_hi: 4, z_lo: 2; z = z_hi * 2 + z_lo), core: 2. Of those that a mesh axis runs over, the one named last changes fastest.
Arguments:
- sim: bfloat16 [7168, 7168], P('row', 'col'), may hold values from 0 to 2304, as said below
- live: int32 [56, 56], P(None, 'col'), may hold values from 0 to 1, as said below
Outputs:
- flow: float32 [7168, 7168], P('row', 'col')
The draws below stay inside these ranges and needn't reach their ends.
Inputs may be any that keep to these rules, and one draw needn't show every extreme that they name: sim is symmetric and nonnegative, with a positive diagonal. live is symmetric, with ones on its diagonal.
All inputs are finite; a program needn't handle non-finite values.
Results may differ from the reference program's by a relative error of at most 0.00067.
Values may be sent and summed in bfloat16 or wider, within the bound.
A program may use at most 128 MiB of HBM per device.

```python
import math
import jax
import jax.numpy as jnp

TILE = 128
NODES = 7168
TILES = 56


def tile_layout(key):
    key_links = jax.random.fold_in(key, 11)
    key_length, key_hubs, key_pairs = jax.random.split(key_links, 3)
    tile_ids = jnp.arange(TILES, dtype=jnp.int32)
    lengths = jax.random.randint(key_length, (TILES,), 1, 5, dtype=jnp.int32)
    cluster_ends = jnp.cumsum(lengths)
    cluster = jnp.sum((cluster_ends[None, :] <= tile_ids[:, None]).astype(jnp.int32), axis=1)
    same_cluster = cluster[:, None] == cluster[None, :]
    hub_flags = (jax.random.randint(key_hubs, (TILES,), 0, 6, dtype=jnp.int32) == 0).astype(jnp.int32)
    link_rate = 25 + 150 * (hub_flags[:, None] + hub_flags[None, :])
    ballot = jax.random.randint(key_pairs, (TILES, TILES), 0, 1000, dtype=jnp.int32)
    upper_links = (ballot < link_rate) & (tile_ids[:, None] < tile_ids[None, :])
    return (same_cluster | upper_links | upper_links.T).astype(jnp.int32)


def draw_live(key, part):
    return tile_layout(key)


def draw_sim(key, part):
    layout = tile_layout(key).astype(jnp.float32)
    key = jax.random.fold_in(key, 7)
    key_values, key_keep, key_scale = jax.random.split(key, 3)
    position = jnp.arange(NODES, dtype=jnp.float32) / NODES
    values = jnp.exp(jax.random.uniform(key_values, (NODES, NODES), jnp.float32, math.log(0.1), 0.0))
    kept = jax.random.uniform(key_keep, (NODES, NODES), jnp.float32) < 0.7
    spread = jnp.exp(jax.random.uniform(key_scale, (NODES,), jnp.float32, 0.0, math.log(10.0)))
    values = jnp.where(kept, values, 0.0)
    row_ids = jnp.arange(NODES, dtype=jnp.int32)[:, None]
    col_ids = jnp.arange(NODES, dtype=jnp.int32)[None, :]
    mirrored = jnp.where(row_ids < col_ids, values, values.T)
    mirrored = jnp.where(row_ids == col_ids, 1.0, mirrored)
    marks = jnp.repeat(jnp.repeat(layout, TILE, axis=0), TILE, axis=1)
    scales = spread * jnp.exp(math.log(3.0) * position)
    return (scales[:, None] * mirrored * scales[None, :] * marks).astype(jnp.bfloat16)


def setup_inputs(seed: int = 0) -> dict:
    key_list = jax.random.split(jax.random.key(seed), 3)
    sim = draw_sim(jax.random.fold_in(key_list[2], 71), 0)
    live = draw_live(jax.random.fold_in(key_list[2], 71), 0)
    return {"sim": sim, "live": live}


def reference(sim, live):
    marks = jnp.repeat(jnp.repeat(live.astype(jnp.bfloat16), TILE, axis=0), TILE, axis=1)
    linked = sim * marks
    degree = jnp.sum(linked.astype(jnp.float32), axis=0)
    weighted = (linked.astype(jnp.float32) / degree[:, None]).astype(jnp.bfloat16)
    expanded = jnp.dot(linked, weighted, preferred_element_type=jnp.float32)
    inflated = expanded * expanded
    total = jnp.sum(inflated, axis=0)
    return NODES * inflated / total[None, :]
```

```python
import jax
import jax.numpy as jnp
from jax import lax
from jax.experimental import pallas as pl
from jax.experimental.pallas import tpu as pltpu
from jax.sharding import PartitionSpec as P

MESH = pl.DeviceIdType.MESH
TILE = 128
STRIP = 32
ROWS = 224
COLS = 896
ROW_DEVICES = 32
COL_DEVICES = 8
NODES = 7168
HALF = 96
TOP, BOTTOM, EDGE, EDGE_TOP, EDGE_BOTTOM = 0, 1, 2, 3, 4
PIECES = {
    TOP: (0, HALF),
    BOTTOM: (HALF, HALF),
    EDGE: (2 * HALF, ROWS - 2 * HALF),
    EDGE_TOP: (2 * HALF, (ROWS - 2 * HALF) // 2),
    EDGE_BOTTOM: (2 * HALF + (ROWS - 2 * HALF) // 2, (ROWS - 2 * HALF) // 2),
}
PANEL_HALF = ROWS // 2
SENDS = 112


def kernel(
    sim_ref,
    live_ref,
    out_ref,
    panel,
    weighted,
    expanded,
    degree_own,
    degree_pair,
    degree_sum,
    degree_in,
    total_own,
    total_core,
    total_x,
    total_z,
    send_sem,
    recv_w,
    recv_core,
    recv_a,
    recv_small,
):
    row, col = lax.axis_index("row"), lax.axis_index("col")
    x, zh, core = row // 8, (row // 2) % 4, row % 2
    zl, y = col // 4, col % 4

    def to_x(d):
        return ((x + d + 4) % 4 * 4 + zh) * 2 + core, col

    def to_z(d):
        return (x * 4 + (zh + d + 4) % 4) * 2 + core, col

    def to_y(d):
        return row, zl * 4 + (y + d + 4) % 4

    to_pair = (row, (1 - zl) * 4 + y)
    to_core = (row + 1 - 2 * core, col)

    barrier = pltpu.get_barrier_semaphore()
    partners = [to(d) for to in (to_x, to_y, to_z) for d in (1, 2, 3)] + [to_pair, to_core]
    for device in partners:
        pl.semaphore_signal(barrier, 1, device_id=device, device_id_type=MESH)

    for s in range(ROWS // STRIP):
        tile_row = (row * (ROWS // STRIP) + s) // (TILE // STRIP)
        for t in range(COLS // TILE):
            mark = live_ref[tile_row, t].astype(jnp.float32)
            strip = sim_ref[s * STRIP : (s + 1) * STRIP, t * TILE : (t + 1) * TILE]
            panel[col, s * STRIP : (s + 1) * STRIP, t * TILE : (t + 1) * TILE] = (
                strip.astype(jnp.float32) * mark
            ).astype(jnp.bfloat16)
    adj = panel[col]
    ones = jnp.ones((8, COLS), jnp.bfloat16)
    sums = lax.dot_general(
        ones, adj, (((1,), (1,)), ((), ())), preferred_element_type=jnp.float32
    )
    degree_own[...] = jnp.zeros_like(degree_own)
    degree_own[:, :ROWS] = sums

    pl.semaphore_wait(barrier, len(partners))

    sends = []

    def send(src, dst, recv, device):
        copy = pltpu.make_async_remote_copy(
            src, dst, send_sem.at[len(sends)], recv, device_id=device, device_id_type=MESH
        )
        copy.start()
        sends.append(copy)

    def arrived(ref, recv):
        pltpu.make_async_remote_copy(
            ref, ref, send_sem.at[0], recv, device_id=to_core, device_id_type=MESH
        ).wait_recv()

    def a_ref(pair, dy, half):
        slot = (zl if pair == 0 else 1 - zl) * 4 + (y + dy + 4) % 4
        return panel.at[slot, pl.ds(half * PANEL_HALF, PANEL_HALF)]

    def a_send_pair(half):
        ref = a_ref(0, 0, half)
        send(ref, ref, recv_a.at[1, 0, half], to_pair)

    def a_send_y(pair, dy, half, step):
        ref = a_ref(pair, dy, half)
        send(ref, ref, recv_a.at[pair, (dy - step) % 4, half], to_y(step))

    def a_wait(pair, dy, half):
        arrived(a_ref(pair, dy, half), recv_a.at[pair, dy % 4, half])

    def w_row(dx, dz, which):
        return (((x + dx + 4) % 4) * 4 + (zh + dz + 4) % 4) * 2 + which

    def w_ref(dx, dz, piece):
        start, size = PIECES[piece]
        first = pl.multiple_of(w_row(dx, dz, core) * ROWS + start, 16)
        return weighted.at[pl.ds(first, size)]

    def w_send(dx, dz, piece, axis, step):
        ref = w_ref(dx, dz, piece)
        nx, nz = (dx - step, dz) if axis == 0 else (dx, dz - step)
        send(
            ref,
            ref,
            recv_w.at[nx % 4, nz % 4, piece],
            to_x(step) if axis == 0 else to_z(step),
        )

    def w_wait(dx, dz, piece):
        arrived(w_ref(dx, dz, piece), recv_w.at[dx % 4, dz % 4, piece])

    def w_block(dx, dz, which):
        return weighted.at[pl.ds(pl.multiple_of(w_row(dx, dz, which) * ROWS, 16), ROWS)]

    def share(dx, dz):
        ref = w_block(dx, dz, core)
        send(ref, ref, recv_core.at[dx % 4, dz % 4], to_core)

    def shared(dx, dz):
        arrived(w_block(dx, dz, 1 - core), recv_core.at[dx % 4, dz % 4])

    send(degree_own, degree_pair, recv_small.at[0], to_pair)
    for half in (0, 1):
        a_send_pair(half)
    for half in (0, 1):
        a_send_y(0, 0, half, 1)
        a_send_y(0, 0, 1 - half, -1)
    arrived(degree_pair, recv_small.at[0])
    degree_sum[...] = degree_own[...] + degree_pair[...]
    for d in (1, 3, 2):
        send(degree_sum, degree_in.at[4 - d], recv_small.at[4 - d], to_y(d))
    degree = degree_sum[...]
    for d in (1, 3, 2):
        arrived(degree_in.at[d], recv_small.at[d])
        degree += degree_in[d]
    degree_column = jnp.transpose(degree)[:ROWS, 0:1]
    own = pl.multiple_of(row * ROWS, 16)
    weighted[pl.ds(own, ROWS), :] = (adj.astype(jnp.float32) / degree_column).astype(
        jnp.bfloat16
    )

    w_send(0, 0, TOP, 1, 1)
    w_send(0, 0, BOTTOM, 1, -1)
    w_send(0, 0, TOP, 0, 1)
    w_send(0, 0, BOTTOM, 0, -1)
    w_send(0, 0, EDGE, 0, 1)
    w_send(0, 0, EDGE, 0, -1)
    w_send(0, 0, BOTTOM, 1, 1)
    w_send(0, 0, TOP, 1, -1)
    w_send(0, 0, BOTTOM, 0, 1)
    w_send(0, 0, TOP, 0, -1)
    w_send(0, 0, EDGE, 1, 1)
    w_send(0, 0, EDGE, 1, -1)
    share(0, 0)

    def along_x(dz, piece):
        w_send(0, dz, piece, 0, 1)
        w_send(0, dz, piece, 0, -1)

    def along_z(dx):
        w_send(dx, 0, EDGE, 1, 1)
        w_send(dx, 0, EDGE, 1, -1)

    def pass_x(dz):
        w_wait(-1, dz, TOP)
        w_send(-1, dz, TOP, 0, 1)
        w_wait(1, dz, BOTTOM)
        w_send(1, dz, BOTTOM, 0, -1)

    def rest_x(dz):
        w_wait(-1, dz, BOTTOM)
        w_wait(1, dz, TOP)

    def last_x(dz):
        w_wait(2, dz, TOP)
        w_wait(2, dz, BOTTOM)

    def pass_z(dx):
        w_wait(dx, -1, EDGE)
        w_send(dx, -1, EDGE_TOP, 1, 1)
        w_wait(dx, 1, EDGE)
        w_send(dx, 1, EDGE_BOTTOM, 1, -1)

    def last_z(dx):
        w_wait(dx, 2, EDGE_TOP)
        w_wait(dx, 2, EDGE_BOTTOM)

    def multiply(dx, first):
        xx = (x + dx) % 4

        for start in range(0, COLS, 256):
            size = min(256, COLS - start)
            acc = None
            for half in (0, 1):
                depth = pl.multiple_of((xx * 2 + half) * COLS, 16)
                part = jnp.dot(
                    panel[xx * 2 + half],
                    weighted[pl.ds(depth, COLS), start : start + size],
                    preferred_element_type=jnp.float32,
                )
                acc = part if acc is None else acc + part
            if first:
                expanded[:, start : start + size] = acc
            else:
                expanded[:, start : start + size] += acc

    w_wait(0, -1, TOP)
    w_send(0, -1, TOP, 1, 1)
    along_x(-1, TOP)
    w_wait(0, 1, BOTTOM)
    w_send(0, 1, BOTTOM, 1, -1)
    along_x(1, BOTTOM)
    pass_x(0)
    w_wait(-1, 0, EDGE)
    w_send(-1, 0, EDGE_TOP, 0, 1)
    along_z(-1)
    w_wait(1, 0, EDGE)
    w_send(1, 0, EDGE_BOTTOM, 0, -1)
    along_z(1)
    for half in (0, 1):
        a_wait(1, 0, half)
        a_send_y(1, 0, half, 1)
        a_send_y(1, 0, half, -1)
    a_wait(0, -1, 0)
    a_send_y(0, -1, 0, 1)
    a_wait(0, 1, 1)
    a_send_y(0, 1, 1, -1)
    w_wait(0, -1, BOTTOM)
    along_x(-1, BOTTOM)
    w_wait(0, 1, TOP)
    along_x(1, TOP)
    rest_x(0)
    share(-1, 0)
    share(1, 0)
    w_wait(2, 0, EDGE_TOP)
    w_wait(2, 0, EDGE_BOTTOM)
    along_z(2)
    last_x(0)
    share(2, 0)
    pass_z(0)
    share(0, -1)
    share(0, 1)
    w_wait(0, 2, TOP)
    along_x(2, TOP)
    w_wait(0, 2, BOTTOM)
    along_x(2, BOTTOM)
    pass_x(-1)
    pass_z(-1)
    pass_x(1)
    pass_z(1)
    last_z(0)
    share(0, 2)
    a_wait(1, -1, 0)
    a_send_y(1, -1, 0, 1)
    a_wait(1, 1, 1)
    a_send_y(1, 1, 1, -1)
    rest_x(-1)
    share(-1, -1)
    share(1, -1)
    rest_x(1)
    share(-1, 1)
    share(1, 1)
    pass_z(2)
    last_x(-1)
    share(2, -1)
    last_x(1)
    share(2, 1)
    pass_x(2)
    for pair in (0, 1):
        for dy, half in ((-1, 1), (1, 0), (2, 0), (2, 1)):
            a_wait(pair, dy, half)
    for dz in (0, -1, 1, 2):
        shared(0, dz)
    multiply(0, True)
    rest_x(2)
    last_z(-1)
    share(-1, 2)
    last_z(1)
    share(1, 2)
    last_z(2)
    last_x(2)
    share(2, 2)
    for dx in (-1, 1, 2):
        for dz in (0, -1, 1, 2):
            shared(dx, dz)
        multiply(dx, False)

    inflated = expanded[...] * expanded[...]
    part = jnp.sum(inflated.reshape(ROWS // 8, 8, COLS), axis=0)
    total_own[0] = part
    send(total_own.at[0], total_core, recv_small.at[4], to_core)
    arrived(total_core, recv_small.at[4])
    part += total_core[...]
    total_own[1] = part
    for d in (1, 3, 2):
        send(total_own.at[1], total_x.at[4 - d], recv_small.at[4 + 4 - d], to_x(d))
    for d in (1, 3, 2):
        arrived(total_x.at[d], recv_small.at[4 + d])
        part += total_x[d]
    total_own[2] = part
    for d in (1, 3, 2):
        send(total_own.at[2], total_z.at[4 - d], recv_small.at[8 + 4 - d], to_z(d))
    for d in (1, 3, 2):
        arrived(total_z.at[d], recv_small.at[8 + d])
        part += total_z[d]
    total = jnp.sum(part, axis=0, keepdims=True)
    out_ref[...] = NODES * inflated / total
    for copy in sends:
        copy.wait_send()


def per_device(sim, live):
    small = pltpu.VMEM((8, 256), jnp.float32)
    wide = (8, COLS)
    return pl.pallas_call(
        kernel,
        out_shape=jax.ShapeDtypeStruct((ROWS, COLS), jnp.float32),
        in_specs=[
            pl.BlockSpec(memory_space=pltpu.VMEM),
            pl.BlockSpec(memory_space=pltpu.SMEM),
        ],
        out_specs=pl.BlockSpec(memory_space=pltpu.VMEM),
        scratch_shapes=[
            pltpu.VMEM((COL_DEVICES, ROWS, COLS), jnp.bfloat16),
            pltpu.VMEM((NODES, COLS), jnp.bfloat16),
            pltpu.VMEM((ROWS, COLS), jnp.float32),
            small,
            small,
            small,
            pltpu.VMEM((4, 8, 256), jnp.float32),
            pltpu.VMEM((3, *wide), jnp.float32),
            pltpu.VMEM(wide, jnp.float32),
            pltpu.VMEM((4, *wide), jnp.float32),
            pltpu.VMEM((4, *wide), jnp.float32),
            pltpu.SemaphoreType.DMA((SENDS,)),
            pltpu.SemaphoreType.DMA((4, 4, 5)),
            pltpu.SemaphoreType.DMA((4, 4)),
            pltpu.SemaphoreType.DMA((2, 4, 2)),
            pltpu.SemaphoreType.DMA((12,)),
        ],
        compiler_params=pltpu.CompilerParams(
            collective_id=0, has_side_effects=True, vmem_limit_bytes=56 * 2**20
        ),
        name="expand_inflate",
    )(sim, live)


def solution(mesh):
    return jax.shard_map(
        per_device,
        mesh=mesh,
        in_specs=(P("row", "col"), P(None, "col")),
        out_specs=P("row", "col"),
        check_vma=False,
    )
```

```python
import functools

import jax
import jax.numpy as jnp
import numpy as np
from jax import lax
from jax.experimental import pallas as pl
from jax.experimental.pallas import tpu as pltpu
from jax.sharding import PartitionSpec as P

MESH = pl.DeviceIdType.MESH
TILE = 128
STRIP = 32
ROWS = 224
COLS = 896
ROW_DEVICES = 32
COL_DEVICES = 8
NODES = 7168
TOP, BOTTOM, EDGE, EDGE_TOP, EDGE_BOTTOM = 0, 1, 2, 3, 4


def parts_of(half, edge):
    return {
        TOP: (0, half),
        BOTTOM: (half, half),
        EDGE: (2 * half, 2 * edge),
        EDGE_TOP: (2 * half, edge),
        EDGE_BOTTOM: (2 * half + edge, edge),
    }


ROW_PARTS = parts_of(96, 16)
SLOTS = 22
SLOT_PARTS = parts_of(9, 2)
STRIPS = ROWS // STRIP
SHARE = 2 * STRIPS
SPOTS = 4 * SHARE
PANEL_HALF = ROWS // 2
SENDS = 112


def place_tables():
    place = np.arange(TILE)
    source, s, u = place // SHARE, place % SHARE // 2, place % 2
    used = place < SPOTS
    tile_rows = np.zeros((8, NODES // TILE, TILE))
    for zh in range(4):
        for core in range(2):
            block = (source * 4 + zh) * 2 + core
            tile = (block * STRIPS + s) // (TILE // STRIP)
            tile_rows[zh * 2 + core] = used & (np.arange(NODES // TILE)[:, None] == tile)
    tile_cols = np.zeros((4, 8, TILE))
    for q in range(4):
        tile_cols[q] = used & (np.arange(8)[:, None] == (q - s) % 4 + 4 * u)
    before = place[:, None] < place[None, :]
    flat = [m.reshape(-1, TILE) for m in (tile_rows, tile_cols, before)]
    return np.concatenate(flat).astype(jnp.bfloat16)


def kernel(sparse, *refs):
    if sparse:
        (sim_ref, live_ref, marks_ref, tables_ref, out_ref, flag_ref, *refs) = refs
        (packed, out_share, in_share, stage, mark, order, table, table_smem, take, take_smem, copy_sem, *refs) = refs
    else:
        sim_ref, live_ref, out_ref, *refs = refs
    (panel, weighted, expanded, degree_own, degree_pair, degree_sum, degree_in, total_own, total_core, total_x, total_z, *refs) = refs
    send_sem, recv_w, recv_core, recv_a, recv_small, recv_share = refs
    row, col = lax.axis_index("row"), lax.axis_index("col")
    x, zh, core = row // 8, (row // 2) % 4, row % 2
    zl, y = col // 4, col % 4

    def to_x(d):
        return ((x + d + 4) % 4 * 4 + zh) * 2 + core, col

    def to_z(d):
        return (x * 4 + (zh + d + 4) % 4) * 2 + core, col

    def to_y(d):
        return row, zl * 4 + (y + d + 4) % 4

    to_pair = (row, (1 - zl) * 4 + y)
    to_core = (row + 1 - 2 * core, col)

    barrier = pltpu.get_barrier_semaphore()
    partners = [to(d) for to in (to_x, to_y, to_z) for d in (1, 2, 3)] + [to_pair, to_core]
    for device in partners:
        pl.semaphore_signal(barrier, 1, device_id=device, device_id_type=MESH)

    for s in range(ROWS // STRIP):
        tile_row = (row * (ROWS // STRIP) + s) // (TILE // STRIP)
        for t in range(COLS // TILE):
            kept = live_ref[t, tile_row].astype(jnp.float32)
            strip = sim_ref[s * STRIP : (s + 1) * STRIP, t * TILE : (t + 1) * TILE]
            panel[col, s * STRIP : (s + 1) * STRIP, t * TILE : (t + 1) * TILE] = (
                strip.astype(jnp.float32) * kept
            ).astype(jnp.bfloat16)
    adj = panel[col]
    ones = jnp.ones((8, COLS), jnp.bfloat16)
    sums = lax.dot_general(
        ones, adj, (((1,), (1,)), ((), ())), preferred_element_type=jnp.float32
    )
    degree_own[...] = jnp.zeros_like(degree_own)
    degree_own[:, :ROWS] = sums

    if sparse:
        marks = marks_ref[...].astype(jnp.float32).astype(jnp.bfloat16)
        tiles = NODES // TILE
        for zc in range(8):
            picked = jnp.dot(
                marks,
                tables_ref[zc * tiles : (zc + 1) * tiles, :],
                preferred_element_type=jnp.float32,
            )
            for q in range(4):
                first = 8 * tiles + q * 8
                columns = tables_ref[first : first + 8, :].astype(jnp.float32)[: COLS // TILE]
                mark[q * 8 + zc : q * 8 + zc + 1, :] = jnp.sum(
                    picked * columns, axis=0, keepdims=True
                )
        live = mark[...]
        before = jnp.dot(
            live.astype(jnp.bfloat16),
            tables_ref[8 * tiles + 32 :, :],
            preferred_element_type=jnp.float32,
        )
        order[...] = before + live
        most = jnp.max(jnp.max(before + live, axis=1, keepdims=True), axis=0, keepdims=True)
        degree_own[:, ROWS:] = jnp.broadcast_to(most, (8, 256 - ROWS))
        table[...] = jnp.where((live > 0) & (before < SLOTS), before, SLOTS).astype(jnp.int32)
        slot = lax.broadcasted_iota(jnp.int32, (32, TILE), 0).astype(jnp.float32)
        spot = lax.broadcasted_iota(jnp.int32, (32, TILE), 1)
        passed = jnp.where((order[pl.ds(row, 1), :] <= slot) & (spot < SPOTS), 1.0, 0.0)
        index = jnp.minimum(jnp.sum(passed, axis=1, keepdims=True), SPOTS - 1.0)
        take[...] = jnp.broadcast_to(index, (32, TILE)).astype(jnp.int32)
        table_copy = pltpu.make_async_copy(table, table_smem, copy_sem.at[0])
        take_copy = pltpu.make_async_copy(take, take_smem, copy_sem.at[1])
        table_copy.start()
        take_copy.start()
        out_share[...] = jnp.zeros_like(out_share)
        stage[SLOTS] = jnp.zeros((STRIP, TILE), jnp.bfloat16)

    pl.semaphore_wait(barrier, len(partners))

    sends = []

    def send(src, dst, recv, device):
        copy = pltpu.make_async_remote_copy(
            src, dst, send_sem.at[len(sends)], recv, device_id=device, device_id_type=MESH
        )
        copy.start()
        sends.append(copy)

    def arrived(ref, recv):
        pltpu.make_async_remote_copy(
            ref, ref, send_sem.at[0], recv, device_id=to_core, device_id_type=MESH
        ).wait_recv()

    def a_ref(pair, dy, half):
        slot = (zl if pair == 0 else 1 - zl) * 4 + (y + dy + 4) % 4
        return panel.at[slot, pl.ds(half * PANEL_HALF, PANEL_HALF)]

    def a_send_pair(half):
        ref = a_ref(0, 0, half)
        send(ref, ref, recv_a.at[1, 0, half], to_pair)

    def a_send_y(pair, dy, half, step):
        ref = a_ref(pair, dy, half)
        send(ref, ref, recv_a.at[pair, (dy - step) % 4, half], to_y(step))

    def a_wait(pair, dy, half):
        arrived(a_ref(pair, dy, half), recv_a.at[pair, dy % 4, half])

    def w_row(dx, dz, which):
        return (((x + dx + 4) % 4) * 4 + (zh + dz + 4) % 4) * 2 + which

    def w_ref(dx, dz, piece):
        if sparse:
            start, size = SLOT_PARTS[piece]
            return packed.at[w_row(dx, dz, core), pl.ds(start, size)]
        start, size = ROW_PARTS[piece]
        first = pl.multiple_of(w_row(dx, dz, core) * ROWS + start, 16)
        return weighted.at[pl.ds(first, size)]

    def w_send(dx, dz, piece, axis, step):
        ref = w_ref(dx, dz, piece)
        nx, nz = (dx - step, dz) if axis == 0 else (dx, dz - step)
        send(
            ref,
            ref,
            recv_w.at[nx % 4, nz % 4, piece],
            to_x(step) if axis == 0 else to_z(step),
        )

    def w_wait(dx, dz, piece):
        arrived(w_ref(dx, dz, piece), recv_w.at[dx % 4, dz % 4, piece])

    def w_block(dx, dz, which):
        if sparse:
            return packed.at[w_row(dx, dz, which)]
        return weighted.at[pl.ds(pl.multiple_of(w_row(dx, dz, which) * ROWS, 16), ROWS)]

    def share(dx, dz):
        ref = w_block(dx, dz, core)
        send(ref, ref, recv_core.at[dx % 4, dz % 4], to_core)

    def shared(dx, dz):
        arrived(w_block(dx, dz, 1 - core), recv_core.at[dx % 4, dz % 4])

    send(degree_own, degree_pair, recv_small.at[0], to_pair)
    for half in (0, 1):
        a_send_pair(half)
    for half in (0, 1):
        a_send_y(0, 0, half, 1)
        a_send_y(0, 0, 1 - half, -1)
    arrived(degree_pair, recv_small.at[0])
    lane = lax.broadcasted_iota(jnp.int32, (8, 256), 1)

    def join(a, b):
        return jnp.where(lane < ROWS, a + b, jnp.maximum(a, b))

    degree_sum[...] = join(degree_own[...], degree_pair[...])
    for d in (1, 3, 2):
        send(degree_sum, degree_in.at[4 - d], recv_small.at[4 - d], to_y(d))
    degree = degree_sum[...]
    for d in (1, 3, 2):
        arrived(degree_in.at[d], recv_small.at[d])
        degree = join(degree, degree_in[d])
    degree_column = jnp.transpose(degree)[:ROWS, 0:1]
    scaled = (adj.astype(jnp.float32) / degree_column).astype(jnp.bfloat16)
    if sparse:
        flag_ref[...] = degree[:, TILE:]
        for q in range(4):
            for s in range(STRIPS):
                for u in (0, 1):
                    t = (q - s) % 4 + 4 * u
                    if t < COLS // TILE:
                        out_share[q, s * 2 + u] = scaled[
                            s * STRIP : (s + 1) * STRIP, t * TILE : (t + 1) * TILE
                        ]
        for d in (2, 1, 3):
            there = (x + d) % 4
            send(out_share.at[there], in_share.at[pl.ds(x * SHARE, SHARE)], recv_share.at[4 - d], to_x(d))
        in_share[pl.ds(x * SHARE, SHARE)] = out_share[x]
        table_copy.wait()
        take_copy.wait()
        for d in (1, 3, 2):
            arrived(in_share.at[pl.ds((x + d) % 4 * SHARE, SHARE)], recv_share.at[d])
        for k in range(SLOTS):
            packed[row, k] = in_share[jnp.clip(take_smem[k, 0], 0, SPOTS - 1)]
    else:
        weighted[pl.ds(pl.multiple_of(row * ROWS, 16), ROWS), :] = scaled

    w_send(0, 0, TOP, 1, 1)
    w_send(0, 0, BOTTOM, 1, -1)
    w_send(0, 0, TOP, 0, 1)
    w_send(0, 0, BOTTOM, 0, -1)
    w_send(0, 0, EDGE, 0, 1)
    w_send(0, 0, EDGE, 0, -1)
    w_send(0, 0, BOTTOM, 1, 1)
    w_send(0, 0, TOP, 1, -1)
    w_send(0, 0, BOTTOM, 0, 1)
    w_send(0, 0, TOP, 0, -1)
    w_send(0, 0, EDGE, 1, 1)
    w_send(0, 0, EDGE, 1, -1)
    share(0, 0)

    def along_x(dz, piece):
        w_send(0, dz, piece, 0, 1)
        w_send(0, dz, piece, 0, -1)

    def along_z(dx):
        w_send(dx, 0, EDGE, 1, 1)
        w_send(dx, 0, EDGE, 1, -1)

    def pass_x(dz):
        w_wait(-1, dz, TOP)
        w_send(-1, dz, TOP, 0, 1)
        w_wait(1, dz, BOTTOM)
        w_send(1, dz, BOTTOM, 0, -1)

    def rest_x(dz):
        w_wait(-1, dz, BOTTOM)
        w_wait(1, dz, TOP)

    def last_x(dz):
        w_wait(2, dz, TOP)
        w_wait(2, dz, BOTTOM)

    def pass_z(dx):
        w_wait(dx, -1, EDGE)
        w_send(dx, -1, EDGE_TOP, 1, 1)
        w_wait(dx, 1, EDGE)
        w_send(dx, 1, EDGE_BOTTOM, 1, -1)

    def last_z(dx):
        w_wait(dx, 2, EDGE_TOP)
        w_wait(dx, 2, EDGE_BOTTOM)

    def unpack(dx, dz, which):
        xx, zz = (x + dx + 4) % 4, (zh + dz + 4) % 4
        block = w_row(dx, dz, which)
        stage[:SLOTS] = packed[block]

        @pl.loop(0, STRIPS)
        def _(s):
            t = (xx - s + 8) % 4
            for source in range(4):
                first = ((source * 4 + zz) * 2 + which) * ROWS + s * STRIP
                for u in (0, 1):
                    slot = table_smem[block, source * SHARE + 2 * s + u]
                    piece = stage[jnp.clip(slot, 0, SLOTS)]
                    weighted[t + 4 * u, pl.ds(pl.multiple_of(first, STRIP), STRIP)] = piece

    pending = []

    def ready(dx, dz):
        share(dx, dz)
        if sparse:
            unpack(dx, dz, core)
            pending.append((dx, dz))
            if len(pending) > 2:
                drain(1)

    def drain(count):
        for _ in range(count):
            dx, dz = pending.pop(0)
            shared(dx, dz)
            unpack(dx, dz, 1 - core)

    def multiply_pair(pair, first):
        for n in range(0, COLS // TILE, 2):
            width = min(2, COLS // TILE - n)
            acc = None
            for source in range(4):
                group = source * 2 + pair
                depth = pl.ds(pl.multiple_of(group * COLS, 16), COLS)
                right = weighted[n, depth]
                if width == 2:
                    right = jnp.concatenate([right, weighted[n + 1, depth]], axis=1)
                part = jnp.dot(panel[group], right, preferred_element_type=jnp.float32)
                acc = part if acc is None else acc + part
            columns = slice(n * TILE, (n + width) * TILE)
            if first:
                expanded[:, columns] = acc
            else:
                expanded[:, columns] += acc

    def multiply(dx, first):
        xx = (x + dx) % 4

        for start in range(0, COLS, 256):
            size = min(256, COLS - start)
            acc = None
            for half in (0, 1):
                depth = pl.multiple_of((xx * 2 + half) * COLS, 16)
                part = jnp.dot(
                    panel[xx * 2 + half],
                    weighted[pl.ds(depth, COLS), start : start + size],
                    preferred_element_type=jnp.float32,
                )
                acc = part if acc is None else acc + part
            if first:
                expanded[:, start : start + size] = acc
            else:
                expanded[:, start : start + size] += acc

    if sparse:
        unpack(0, 0, core)
        pending.append((0, 0))
    w_wait(0, -1, TOP)
    w_send(0, -1, TOP, 1, 1)
    along_x(-1, TOP)
    w_wait(0, 1, BOTTOM)
    w_send(0, 1, BOTTOM, 1, -1)
    along_x(1, BOTTOM)
    pass_x(0)
    w_wait(-1, 0, EDGE)
    w_send(-1, 0, EDGE_TOP, 0, 1)
    along_z(-1)
    w_wait(1, 0, EDGE)
    w_send(1, 0, EDGE_BOTTOM, 0, -1)
    along_z(1)
    for half in (0, 1):
        a_wait(1, 0, half)
        a_send_y(1, 0, half, 1)
        a_send_y(1, 0, half, -1)
    a_wait(0, -1, 0)
    a_send_y(0, -1, 0, 1)
    a_wait(0, 1, 1)
    a_send_y(0, 1, 1, -1)
    w_wait(0, -1, BOTTOM)
    along_x(-1, BOTTOM)
    w_wait(0, 1, TOP)
    along_x(1, TOP)
    rest_x(0)
    ready(-1, 0)
    ready(1, 0)
    w_wait(2, 0, EDGE_TOP)
    w_wait(2, 0, EDGE_BOTTOM)
    along_z(2)
    last_x(0)
    ready(2, 0)
    pass_z(0)
    ready(0, -1)
    ready(0, 1)
    w_wait(0, 2, TOP)
    along_x(2, TOP)
    w_wait(0, 2, BOTTOM)
    along_x(2, BOTTOM)
    pass_x(-1)
    pass_z(-1)
    pass_x(1)
    pass_z(1)
    last_z(0)
    ready(0, 2)
    a_wait(1, -1, 0)
    a_send_y(1, -1, 0, 1)
    a_wait(1, 1, 1)
    a_send_y(1, 1, 1, -1)
    rest_x(-1)
    ready(-1, -1)
    ready(1, -1)
    rest_x(1)
    ready(-1, 1)
    ready(1, 1)
    pass_z(2)
    last_x(-1)
    ready(2, -1)
    last_x(1)
    ready(2, 1)
    pass_x(2)
    for pair in (0, 1):
        for dy, half in ((-1, 1), (1, 0), (2, 0), (2, 1)):
            a_wait(pair, dy, half)
    if sparse:
        drain(len(pending))
        multiply_pair(zh // 2, True)
    else:
        for dz in (0, -1, 1, 2):
            shared(0, dz)
        multiply(0, True)
    rest_x(2)
    last_z(-1)
    ready(-1, 2)
    last_z(1)
    ready(1, 2)
    last_z(2)
    last_x(2)
    ready(2, 2)
    if sparse:
        drain(len(pending))
        multiply_pair(1 - zh // 2, False)
    else:
        for dx in (-1, 1, 2):
            for dz in (0, -1, 1, 2):
                shared(dx, dz)
            multiply(dx, False)

    inflated = expanded[...] * expanded[...]
    part = jnp.sum(inflated, axis=0, keepdims=True)
    for t in range(COLS // TILE):
        total_own[0, t : t + 1, :] = part[:, t * TILE : (t + 1) * TILE]
    send(total_own.at[0], total_core, recv_small.at[4], to_core)
    arrived(total_core, recv_small.at[4])
    total_own[1] = total_own[0] + total_core[...]
    for d in (2, 1, 3):
        send(total_own.at[1], total_x.at[4 - d], recv_small.at[4 + 4 - d], to_x(d))
    part = total_own[1]
    for d in (1, 3, 2):
        arrived(total_x.at[d], recv_small.at[4 + d])
        part += total_x[d]
    total_own[2] = part
    for d in (2, 1, 3):
        send(total_own.at[2], total_z.at[4 - d], recv_small.at[8 + 4 - d], to_z(d))
    for d in (1, 3, 2):
        arrived(total_z.at[d], recv_small.at[8 + d])
        part += total_z[d]
    for t in range(COLS // TILE):
        columns = slice(t * TILE, (t + 1) * TILE)
        out_ref[:, columns] = NODES * inflated[:, columns] / part[t : t + 1, :]
    for copy in sends:
        copy.wait_send()


def call(sparse, *operands):
    vmem, sem = pltpu.VMEM, pltpu.SemaphoreType.DMA
    bf16, f32, i32 = jnp.bfloat16, jnp.float32, jnp.int32
    small, tile, table = (8, 256), (8, TILE), (32, TILE)
    flow = jax.ShapeDtypeStruct((ROWS, COLS), f32)
    in_vmem = pl.BlockSpec(memory_space=vmem)
    extra = []
    if sparse:
        extra = [
            vmem((ROW_DEVICES, SLOTS, STRIP, TILE), bf16),
            vmem((4, SHARE, STRIP, TILE), bf16),
            vmem((SPOTS, STRIP, TILE), bf16),
            vmem((SLOTS + 1, STRIP, TILE), bf16),
            vmem(table, f32),
            vmem(table, f32),
            vmem(table, i32),
            pltpu.SMEM(table, i32),
            vmem(table, i32),
            pltpu.SMEM(table, i32),
            sem((2,)),
        ]
    return pl.pallas_call(
        functools.partial(kernel, sparse),
        out_shape=[flow, jax.ShapeDtypeStruct(tile, f32)] if sparse else flow,
        in_specs=[in_vmem, pl.BlockSpec(memory_space=pltpu.SMEM)] + [in_vmem] * (len(operands) - 2),
        out_specs=[in_vmem, in_vmem] if sparse else in_vmem,
        scratch_shapes=[
            *extra,
            vmem((COL_DEVICES, ROWS, COLS), bf16),
            vmem((8, NODES, TILE) if sparse else (NODES, COLS), bf16),
            vmem((ROWS, COLS), f32),
            vmem(small, f32),
            vmem(small, f32),
            vmem(small, f32),
            vmem((4, *small), f32),
            vmem((3, *tile), f32),
            vmem(tile, f32),
            vmem((4, *tile), f32),
            vmem((4, *tile), f32),
            sem((SENDS,)),
            sem((4, 4, 5)),
            sem((4, 4)),
            sem((2, 4, 2)),
            sem((12,)),
            sem((4,)),
        ],
        compiler_params=pltpu.CompilerParams(
            collective_id=0 if sparse else 1,
            has_side_effects=True,
            vmem_limit_bytes=40 * 2**20,
        ),
        name="flow_of_packed" if sparse else "flow_of_whole",
    )(*operands)


def per_device(sim, live):
    marks = live.T
    flow, most = call(True, sim, marks, marks, jnp.asarray(place_tables()))
    return lax.cond(
        most[0, TILE - 1] <= SLOTS, lambda: flow, lambda: call(False, sim, marks)
    )


def solution(mesh):
    return jax.shard_map(
        per_device,
        mesh=mesh,
        in_specs=(P("row", "col"), P(None, "col")),
        out_specs=P("row", "col"),
        check_vma=False,
    )
```

```python
import functools

import jax
import jax.numpy as jnp
import numpy as np
from jax import lax
from jax.experimental import pallas as pl
from jax.experimental.pallas import tpu as pltpu
from jax.sharding import PartitionSpec as P

MESH = pl.DeviceIdType.MESH
TILE = 128
STRIP = 32
ROWS = 224
COLS = 896
ROW_DEVICES = 32
COL_DEVICES = 8
NODES = 7168
TOP, BOTTOM, EDGE, EDGE_TOP, EDGE_BOTTOM = 0, 1, 2, 3, 4


def parts_of(half, edge):
    return {
        TOP: (0, half),
        BOTTOM: (half, half),
        EDGE: (2 * half, 2 * edge),
        EDGE_TOP: (2 * half, edge),
        EDGE_BOTTOM: (2 * half + edge, edge),
    }


ROW_PARTS = parts_of(96, 16)
SLOTS = 22
SLOT_PARTS = parts_of(9, 2)
STRIPS = ROWS // STRIP
SHARE = 2 * STRIPS
SPOTS = 4 * SHARE
PANEL_HALF = ROWS // 2
SENDS = 112


WEIGHTED, PANEL, SHARED, UNPACK, MULTIPLY = range(5)
ORDER = (
    (1, 1, 0, 0), (1, 0, 3, 0), (1, 0, 1, 1), (1, 1, 0, 1), (1, 0, 3, 1), (1, 0, 1, 0), (3, 0, 0, 0), (3, 0, 0, 1),
    (0, 3, 0, 0), (0, 1, 0, 1), (0, 3, 0, 2), (0, 1, 0, 2), (0, 0, 3, 0), (0, 0, 1, 1), (0, 3, 0, 1), (2, 3, 0, 0),
    (0, 1, 0, 0), (2, 1, 0, 0), (3, 3, 0, 0), (3, 1, 0, 0), (1, 1, 3, 0), (1, 0, 2, 1), (0, 2, 0, 0), (0, 2, 0, 1),
    (0, 2, 0, 3), (0, 2, 0, 4), (2, 2, 0, 0), (3, 2, 0, 0), (3, 3, 0, 1), (3, 1, 0, 1), (0, 0, 3, 1), (0, 0, 1, 0),
    (0, 3, 3, 0), (0, 1, 3, 0), (3, 2, 0, 1), (0, 3, 1, 1), (0, 1, 1, 1), (1, 0, 2, 0), (1, 1, 1, 1), (0, 0, 2, 0),
    (0, 0, 2, 1), (0, 3, 3, 1), (0, 1, 3, 1), (0, 0, 3, 2), (2, 0, 3, 0), (0, 0, 1, 2), (2, 0, 1, 0), (3, 0, 3, 0),
    (3, 0, 1, 0), (0, 3, 1, 0), (0, 1, 1, 0), (0, 3, 3, 2), (2, 3, 3, 0), (0, 3, 1, 2), (2, 3, 1, 0), (3, 3, 3, 0),
    (3, 3, 1, 0), (3, 0, 3, 1), (1, 1, 2, 0), (0, 2, 3, 0), (0, 2, 1, 1), (0, 1, 3, 2), (2, 1, 3, 0), (1, 1, 1, 0),
    (0, 1, 1, 2), (2, 1, 1, 0), (3, 0, 1, 1), (3, 1, 3, 0), (3, 1, 1, 0), (0, 2, 3, 3), (0, 2, 1, 3), (3, 3, 3, 1),
    (3, 3, 1, 1), (0, 3, 2, 0), (0, 2, 3, 4), (0, 1, 2, 0), (0, 2, 1, 4), (0, 0, 2, 3), (0, 0, 2, 4), (2, 0, 2, 0),
    (3, 1, 3, 1), (3, 0, 2, 0), (3, 1, 1, 1), (0, 3, 2, 3), (0, 3, 2, 4), (0, 3, 2, 1), (2, 3, 2, 0), (0, 1, 2, 1),
    (3, 3, 2, 0), (0, 1, 2, 3), (0, 1, 2, 4), (2, 1, 2, 0), (3, 1, 2, 0), (1, 1, 3, 1), (0, 2, 2, 3), (1, 1, 2, 1),
    (0, 2, 1, 0), (2, 2, 1, 0), (0, 2, 3, 1), (2, 2, 3, 0), (0, 2, 2, 4), (3, 0, 2, 1), (3, 2, 1, 0), (3, 2, 3, 0),
    (3, 3, 2, 1), (3, 1, 2, 1), (0, 2, 2, 0), (0, 2, 2, 1), (2, 2, 2, 0), (3, 2, 1, 1), (3, 2, 3, 1), (4, 0, 0, 0),
    (3, 2, 2, 0), (3, 2, 2, 1), (4, 1, 0, 0),
)


def place_tables():
    place = np.arange(TILE)
    source, s, u = place // SHARE, place % SHARE // 2, place % 2
    used = place < SPOTS
    tile_rows = np.zeros((8, NODES // TILE, TILE))
    for zh in range(4):
        for core in range(2):
            block = (source * 4 + zh) * 2 + core
            tile = (block * STRIPS + s) // (TILE // STRIP)
            tile_rows[zh * 2 + core] = used & (np.arange(NODES // TILE)[:, None] == tile)
    tile_cols = np.zeros((4, 8, TILE))
    for q in range(4):
        tile_cols[q] = used & (np.arange(8)[:, None] == (q - s) % 4 + 4 * u)
    before = place[:, None] < place[None, :]
    flat = [m.reshape(-1, TILE) for m in (tile_rows, tile_cols, before)]
    return np.concatenate(flat).astype(jnp.bfloat16)


def kernel(sparse, *refs):
    if sparse:
        (sim_ref, live_ref, marks_ref, tables_ref, out_ref, flag_ref, *refs) = refs
        (packed, out_share, in_share, stage, mark, order, table, table_smem, take, take_smem, copy_sem, degree_x, *refs) = refs
    else:
        sim_ref, live_ref, out_ref, *refs = refs
    (panel, weighted, expanded, degree_own, degree_pair, degree_sum, degree_in, total_own, total_core, total_x, total_z, *refs) = refs
    send_sem, recv_w, recv_core, recv_a, recv_small, recv_share = refs
    row, col = lax.axis_index("row"), lax.axis_index("col")
    x, zh, core = row // 8, (row // 2) % 4, row % 2
    zl, y = col // 4, col % 4

    def to_x(d):
        return ((x + d + 4) % 4 * 4 + zh) * 2 + core, col

    def to_z(d):
        return (x * 4 + (zh + d + 4) % 4) * 2 + core, col

    def to_y(d):
        return row, zl * 4 + (y + d + 4) % 4

    to_pair = (row, (1 - zl) * 4 + y)
    to_core = (row + 1 - 2 * core, col)

    barrier = pltpu.get_barrier_semaphore()
    partners = [to(d) for to in (to_x, to_y, to_z) for d in (1, 2, 3)] + [to_pair, to_core]
    for device in partners:
        pl.semaphore_signal(barrier, 1, device_id=device, device_id_type=MESH)

    for s in range(ROWS // STRIP):
        tile_row = (row * (ROWS // STRIP) + s) // (TILE // STRIP)
        for t in range(COLS // TILE):
            kept = live_ref[t, tile_row].astype(jnp.float32)
            strip = sim_ref[s * STRIP : (s + 1) * STRIP, t * TILE : (t + 1) * TILE]
            panel[col, s * STRIP : (s + 1) * STRIP, t * TILE : (t + 1) * TILE] = (
                strip.astype(jnp.float32) * kept
            ).astype(jnp.bfloat16)
    adj = panel[col]
    ones = jnp.ones((8, COLS), jnp.bfloat16)
    sums = lax.dot_general(
        ones, adj, (((1,), (1,)), ((), ())), preferred_element_type=jnp.float32
    )
    degree_own[...] = jnp.zeros_like(degree_own)
    degree_own[:, :ROWS] = sums

    if sparse:
        marks = marks_ref[...].astype(jnp.float32).astype(jnp.bfloat16)
        tiles = NODES // TILE
        for zc in range(8):
            picked = jnp.dot(
                marks,
                tables_ref[zc * tiles : (zc + 1) * tiles, :],
                preferred_element_type=jnp.float32,
            )
            for q in range(4):
                first = 8 * tiles + q * 8
                columns = tables_ref[first : first + 8, :].astype(jnp.float32)[: COLS // TILE]
                mark[q * 8 + zc : q * 8 + zc + 1, :] = jnp.sum(
                    picked * columns, axis=0, keepdims=True
                )
        live = mark[...]
        before = jnp.dot(
            live.astype(jnp.bfloat16),
            tables_ref[8 * tiles + 32 :, :],
            preferred_element_type=jnp.float32,
        )
        order[...] = before + live
        most = jnp.max(jnp.max(before + live, axis=1, keepdims=True), axis=0, keepdims=True)
        degree_own[:, ROWS:] = jnp.broadcast_to(most, (8, 256 - ROWS))
        table[...] = jnp.where((live > 0) & (before < SLOTS), before, SLOTS).astype(jnp.int32)
        slot = lax.broadcasted_iota(jnp.int32, (32, TILE), 0).astype(jnp.float32)
        spot = lax.broadcasted_iota(jnp.int32, (32, TILE), 1)
        passed = jnp.where((order[pl.ds(row, 1), :] <= slot) & (spot < SPOTS), 1.0, 0.0)
        index = jnp.minimum(jnp.sum(passed, axis=1, keepdims=True), SPOTS - 1.0)
        take[...] = jnp.broadcast_to(index, (32, TILE)).astype(jnp.int32)
        table_copy = pltpu.make_async_copy(table, table_smem, copy_sem.at[0])
        take_copy = pltpu.make_async_copy(take, take_smem, copy_sem.at[1])
        table_copy.start()
        take_copy.start()
        out_share[...] = jnp.zeros_like(out_share)
        for q in range(4):
            for s in range(STRIPS):
                for u in (0, 1):
                    t = (q - s) % 4 + 4 * u
                    if t < COLS // TILE:
                        out_share[q, s * 2 + u] = adj[
                            s * STRIP : (s + 1) * STRIP, t * TILE : (t + 1) * TILE
                        ]
        stage[SLOTS] = jnp.zeros((STRIP, TILE), jnp.bfloat16)

    pl.semaphore_wait(barrier, len(partners))

    sends = []

    def send(src, dst, recv, device):
        copy = pltpu.make_async_remote_copy(
            src, dst, send_sem.at[len(sends)], recv, device_id=device, device_id_type=MESH
        )
        copy.start()
        sends.append(copy)

    def arrived(ref, recv):
        pltpu.make_async_remote_copy(
            ref, ref, send_sem.at[0], recv, device_id=to_core, device_id_type=MESH
        ).wait_recv()

    def a_ref(pair, dy, half):
        slot = (zl if pair == 0 else 1 - zl) * 4 + (y + dy + 4) % 4
        return panel.at[slot, pl.ds(half * PANEL_HALF, PANEL_HALF)]

    def a_send_pair(half):
        ref = a_ref(0, 0, half)
        send(ref, ref, recv_a.at[1, 0, half], to_pair)

    def a_send_y(pair, dy, half, step):
        ref = a_ref(pair, dy, half)
        send(ref, ref, recv_a.at[pair, (dy - step) % 4, half], to_y(step))

    def a_wait(pair, dy, half):
        arrived(a_ref(pair, dy, half), recv_a.at[pair, dy % 4, half])

    def w_row(dx, dz, which):
        return (((x + dx + 4) % 4) * 4 + (zh + dz + 4) % 4) * 2 + which

    def w_ref(dx, dz, piece):
        if sparse:
            start, size = SLOT_PARTS[piece]
            return packed.at[w_row(dx, dz, core), pl.ds(start, size)]
        start, size = ROW_PARTS[piece]
        first = pl.multiple_of(w_row(dx, dz, core) * ROWS + start, 16)
        return weighted.at[pl.ds(first, size)]

    def w_send(dx, dz, piece, axis, step):
        ref = w_ref(dx, dz, piece)
        nx, nz = (dx - step, dz) if axis == 0 else (dx, dz - step)
        send(
            ref,
            ref,
            recv_w.at[nx % 4, nz % 4, piece],
            to_x(step) if axis == 0 else to_z(step),
        )

    def w_wait(dx, dz, piece):
        arrived(w_ref(dx, dz, piece), recv_w.at[dx % 4, dz % 4, piece])

    def w_block(dx, dz, which):
        if sparse:
            return packed.at[w_row(dx, dz, which)]
        return weighted.at[pl.ds(pl.multiple_of(w_row(dx, dz, which) * ROWS, 16), ROWS)]

    def share(dx, dz):
        ref = w_block(dx, dz, core)
        send(ref, ref, recv_core.at[dx % 4, dz % 4], to_core)

    def shared(dx, dz):
        arrived(w_block(dx, dz, 1 - core), recv_core.at[dx % 4, dz % 4])

    send(degree_own, degree_pair, recv_small.at[0], to_pair)
    if sparse:
        for d in (2, 1, 3):
            there = (x + d) % 4
            send(out_share.at[there], in_share.at[pl.ds(x * SHARE, SHARE)], recv_share.at[4 - d], to_x(d))
    for half in (0, 1):
        a_send_pair(half)
    arrived(degree_pair, recv_small.at[0])
    lane = lax.broadcasted_iota(jnp.int32, (8, 256), 1)

    def join(a, b):
        return jnp.where(lane < ROWS, a + b, jnp.maximum(a, b))

    degree_sum[...] = join(degree_own[...], degree_pair[...])
    for d in (1, 3, 2):
        send(degree_sum, degree_in.at[4 - d], recv_small.at[4 - d], to_y(d))
    for half in (0, 1):
        a_send_y(0, 0, half, 1)
        a_send_y(0, 0, 1 - half, -1)
    degree = degree_sum[...]
    for d in (1, 3, 2):
        arrived(degree_in.at[d], recv_small.at[d])
        degree = join(degree, degree_in[d])
    if sparse:
        flag_ref[...] = degree[:, TILE:]
        degree_x[0] = degree
        for d in (2, 1, 3):
            send(degree_x.at[0], degree_x.at[4 - d], recv_small.at[16 - d], to_x(d))
        in_share[pl.ds(x * SHARE, SHARE)] = out_share[x]
        table_copy.wait()
        take_copy.wait()
        for d in (0, 1, 3, 2):
            source = (x + d) % 4
            if d:
                arrived(in_share.at[pl.ds(source * SHARE, SHARE)], recv_share.at[d])
                arrived(degree_x.at[d], recv_small.at[12 + d])
            degree_column = jnp.transpose(degree_x[d])[:ROWS, 0:1]
            for s in range(STRIPS):
                column = degree_column[s * STRIP : (s + 1) * STRIP]
                for u in (0, 1):
                    place = source * SHARE + 2 * s + u
                    piece = in_share[place].astype(jnp.float32)
                    in_share[place] = (piece / column).astype(jnp.bfloat16)
        for k in range(SLOTS):
            packed[row, k] = in_share[jnp.clip(take_smem[k, 0], 0, SPOTS - 1)]
    else:
        degree_column = jnp.transpose(degree)[:ROWS, 0:1]
        scaled = (adj.astype(jnp.float32) / degree_column).astype(jnp.bfloat16)
        weighted[pl.ds(pl.multiple_of(row * ROWS, 16), ROWS), :] = scaled

    w_send(0, 0, TOP, 1, 1)
    w_send(0, 0, BOTTOM, 1, -1)
    w_send(0, 0, TOP, 0, 1)
    w_send(0, 0, BOTTOM, 0, -1)
    w_send(0, 0, EDGE, 0, 1)
    w_send(0, 0, EDGE, 0, -1)
    w_send(0, 0, BOTTOM, 1, 1)
    w_send(0, 0, TOP, 1, -1)
    w_send(0, 0, BOTTOM, 0, 1)
    w_send(0, 0, TOP, 0, -1)
    share(0, 0)

    late = []

    def edge_along_z(dx, piece):
        if late is None:
            w_send(dx, 0, piece, 1, 1)
            w_send(dx, 0, piece, 1, -1)
        else:
            late.append((dx, piece))

    def weighted_arrived(dx, dz, piece):
        nonlocal late
        w_wait(dx, dz, piece)
        if dz == 0 and piece > BOTTOM:
            if (dx, piece) in ((3, EDGE), (1, EDGE)):
                w_send(dx, 0, EDGE_TOP if dx == 3 else EDGE_BOTTOM, 0, dx - 2)
            edge_along_z(dx, piece)
        elif piece > BOTTOM:
            if dz == 3 and piece != EDGE_BOTTOM:
                w_send(dx, dz, EDGE_TOP, 1, 1)
            if dz == 1 and piece != EDGE_TOP:
                w_send(dx, dz, EDGE_BOTTOM, 1, -1)
        elif dx == 0:
            if (dz, piece) in ((3, TOP), (1, BOTTOM)):
                w_send(0, dz, piece, 1, dz - 2)
            w_send(0, dz, piece, 0, 1)
            w_send(0, dz, piece, 0, -1)
        elif (dx, piece) in ((3, TOP), (1, BOTTOM)):
            w_send(dx, dz, piece, 0, dx - 2)
        if (dx, dz, piece) == (0, 3, BOTTOM):
            held, late = late, None
            for item in held:
                edge_along_z(*item)

    def panel_arrived(pair, dy, half):
        a_wait(pair, dy, half)
        if (pair, dy) == (1, 0):
            a_send_y(1, 0, half, 1 - 2 * half)
        if (pair, dy) == (0, 2):
            a_send_y(1, 0, 1 - half, 1 - 2 * half)
        if (dy, half) in ((3, 0), (1, 1)):
            a_send_y(pair, dy, half, dy - 2)

    def unpack(dx, dz, which):
        xx, zz = (x + dx + 4) % 4, (zh + dz + 4) % 4
        block = w_row(dx, dz, which)
        stage[:SLOTS] = packed[block]

        @pl.loop(0, STRIPS)
        def _(s):
            t = (xx - s + 8) % 4
            for source in range(4):
                first = ((source * 4 + zz) * 2 + which) * ROWS + s * STRIP
                for u in (0, 1):
                    slot = table_smem[block, source * SHARE + 2 * s + u]
                    piece = stage[jnp.clip(slot, 0, SLOTS)]
                    weighted[t + 4 * u, pl.ds(pl.multiple_of(first, STRIP), STRIP)] = piece

    def multiply_pair(pair, first):
        for n in range(0, COLS // TILE, 2):
            width = min(2, COLS // TILE - n)
            acc = None
            for source in range(4):
                group = source * 2 + pair
                depth = pl.ds(pl.multiple_of(group * COLS, 16), COLS)
                right = weighted[n, depth]
                if width == 2:
                    right = jnp.concatenate([right, weighted[n + 1, depth]], axis=1)
                part = jnp.dot(panel[group], right, preferred_element_type=jnp.float32)
                acc = part if acc is None else acc + part
            columns = slice(n * TILE, (n + width) * TILE)
            if first:
                expanded[:, columns] = acc
            else:
                expanded[:, columns] += acc

    def multiply(dx, first):
        xx = (x + dx) % 4

        for start in range(0, COLS, 256):
            size = min(256, COLS - start)
            acc = None
            for half in (0, 1):
                depth = pl.multiple_of((xx * 2 + half) * COLS, 16)
                part = jnp.dot(
                    panel[xx * 2 + half],
                    weighted[pl.ds(depth, COLS), start : start + size],
                    preferred_element_type=jnp.float32,
                )
                acc = part if acc is None else acc + part
            if first:
                expanded[:, start : start + size] = acc
            else:
                expanded[:, start : start + size] += acc

    edge_along_z(0, EDGE)
    for act, first, second, third in ORDER:
        if act == WEIGHTED:
            weighted_arrived(first, second, third)
        elif act == PANEL:
            panel_arrived(first, second, third)
        elif act == SHARED:
            share(first, second)
        elif act == UNPACK:
            if third:
                shared(first, second)
            if sparse:
                unpack(first, second, 1 - core if third else core)
        elif sparse:
            multiply_pair((zh // 2 + first) % 2, first == 0)
    if not sparse:
        for dx in range(4):
            multiply(dx, dx == 0)

    inflated = expanded[...] * expanded[...]
    part = jnp.sum(inflated, axis=0, keepdims=True)
    for t in range(COLS // TILE):
        total_own[0, t : t + 1, :] = part[:, t * TILE : (t + 1) * TILE]
    send(total_own.at[0], total_core, recv_small.at[4], to_core)
    arrived(total_core, recv_small.at[4])
    total_own[1] = total_own[0] + total_core[...]
    for d in (2, 1, 3):
        send(total_own.at[1], total_x.at[4 - d], recv_small.at[4 + 4 - d], to_x(d))
    part = total_own[1]
    for d in (1, 3, 2):
        arrived(total_x.at[d], recv_small.at[4 + d])
        part += total_x[d]
    total_own[2] = part
    for d in (2, 1, 3):
        send(total_own.at[2], total_z.at[4 - d], recv_small.at[8 + 4 - d], to_z(d))
    for d in (1, 3, 2):
        arrived(total_z.at[d], recv_small.at[8 + d])
        part += total_z[d]
    for t in range(COLS // TILE):
        columns = slice(t * TILE, (t + 1) * TILE)
        out_ref[:, columns] = NODES * inflated[:, columns] / part[t : t + 1, :]
    for copy in sends:
        copy.wait_send()


def call(sparse, *operands):
    vmem, sem = pltpu.VMEM, pltpu.SemaphoreType.DMA
    bf16, f32, i32 = jnp.bfloat16, jnp.float32, jnp.int32
    small, tile, table = (8, 256), (8, TILE), (32, TILE)
    flow = jax.ShapeDtypeStruct((ROWS, COLS), f32)
    in_vmem = pl.BlockSpec(memory_space=vmem)
    extra = []
    if sparse:
        extra = [
            vmem((ROW_DEVICES, SLOTS, STRIP, TILE), bf16),
            vmem((4, SHARE, STRIP, TILE), bf16),
            vmem((SPOTS, STRIP, TILE), bf16),
            vmem((SLOTS + 1, STRIP, TILE), bf16),
            vmem(table, f32),
            vmem(table, f32),
            vmem(table, i32),
            pltpu.SMEM(table, i32),
            vmem(table, i32),
            pltpu.SMEM(table, i32),
            sem((2,)),
            vmem((4, *small), f32),
        ]
    return pl.pallas_call(
        functools.partial(kernel, sparse),
        out_shape=[flow, jax.ShapeDtypeStruct(tile, f32)] if sparse else flow,
        in_specs=[in_vmem, pl.BlockSpec(memory_space=pltpu.SMEM)] + [in_vmem] * (len(operands) - 2),
        out_specs=[in_vmem, in_vmem] if sparse else in_vmem,
        scratch_shapes=[
            *extra,
            vmem((COL_DEVICES, ROWS, COLS), bf16),
            vmem((8, NODES, TILE) if sparse else (NODES, COLS), bf16),
            vmem((ROWS, COLS), f32),
            vmem(small, f32),
            vmem(small, f32),
            vmem(small, f32),
            vmem((4, *small), f32),
            vmem((3, *tile), f32),
            vmem(tile, f32),
            vmem((4, *tile), f32),
            vmem((4, *tile), f32),
            sem((SENDS,)),
            sem((4, 4, 5)),
            sem((4, 4)),
            sem((2, 4, 2)),
            sem((16,)),
            sem((4,)),
        ],
        compiler_params=pltpu.CompilerParams(
            collective_id=0 if sparse else 1,
            has_side_effects=True,
            vmem_limit_bytes=40 * 2**20,
        ),
        name="flow_of_packed" if sparse else "flow_of_whole",
    )(*operands)


def per_device(sim, live):
    marks = live.T
    flow, most = call(True, sim, marks, marks, jnp.asarray(place_tables()))
    return lax.cond(
        most[0, TILE - 1] <= SLOTS, lambda: flow, lambda: call(False, sim, marks)
    )


def solution(mesh):
    return jax.shard_map(
        per_device,
        mesh=mesh,
        in_specs=(P("row", "col"), P(None, "col")),
        out_specs=P("row", "col"),
        check_vma=False,
    )
```

```python
import functools

import jax
import jax.numpy as jnp
import numpy as np
from jax import lax
from jax.experimental import pallas as pl
from jax.experimental.pallas import tpu as pltpu
from jax.sharding import PartitionSpec as P

MESH = pl.DeviceIdType.MESH
TILE = 128
STRIP = 32
ROWS = 224
COLS = 896
ROW_DEVICES = 32
COL_DEVICES = 8
NODES = 7168
TOP, BOTTOM, EDGE, EDGE_TOP, EDGE_BOTTOM = 0, 1, 2, 3, 4


def parts_of(half, edge):
    return {
        TOP: (0, half),
        BOTTOM: (half, half),
        EDGE: (2 * half, 2 * edge),
        EDGE_TOP: (2 * half, edge),
        EDGE_BOTTOM: (2 * half + edge, edge),
    }


ROW_PARTS = parts_of(96, 16)
SLOTS = 22
SLOT_PARTS = parts_of(9, 2)
STRIPS = ROWS // STRIP
SHARE = 2 * STRIPS
SPOTS = 4 * SHARE
PANEL_HALF = ROWS // 2
SENDS = 128


WEIGHTED, PANEL, SHARED, UNPACK, MULTIPLY = range(5)
ORDER = (
    (1, 1, 0, 0), (1, 0, 3, 0), (1, 0, 1, 1), (1, 1, 0, 1), (1, 0, 3, 1), (1, 0, 1, 0), (3, 0, 0, 0), (3, 0, 0, 1),
    (0, 3, 0, 0), (0, 1, 0, 1), (0, 3, 0, 2), (0, 1, 0, 2), (0, 0, 3, 0), (0, 0, 1, 1), (0, 3, 0, 1), (2, 3, 0, 0),
    (0, 1, 0, 0), (2, 1, 0, 0), (3, 3, 0, 0), (3, 1, 0, 0), (1, 1, 3, 0), (1, 0, 2, 1), (0, 2, 0, 0), (0, 2, 0, 1),
    (0, 2, 0, 3), (0, 2, 0, 4), (2, 2, 0, 0), (3, 2, 0, 0), (3, 3, 0, 1), (3, 1, 0, 1), (0, 0, 3, 1), (0, 0, 1, 0),
    (0, 3, 3, 0), (0, 1, 3, 0), (3, 2, 0, 1), (0, 3, 1, 1), (0, 1, 1, 1), (1, 0, 2, 0), (1, 1, 1, 1), (0, 0, 2, 0),
    (0, 0, 2, 1), (0, 3, 3, 1), (0, 1, 3, 1), (0, 0, 3, 2), (2, 0, 3, 0), (0, 0, 1, 2), (2, 0, 1, 0), (3, 0, 3, 0),
    (3, 0, 1, 0), (0, 3, 1, 0), (0, 1, 1, 0), (0, 3, 3, 2), (2, 3, 3, 0), (0, 3, 1, 2), (2, 3, 1, 0), (3, 3, 3, 0),
    (3, 3, 1, 0), (3, 0, 3, 1), (1, 1, 2, 0), (0, 2, 3, 0), (0, 2, 1, 1), (0, 1, 3, 2), (2, 1, 3, 0), (1, 1, 1, 0),
    (0, 1, 1, 2), (2, 1, 1, 0), (3, 0, 1, 1), (3, 1, 3, 0), (3, 1, 1, 0), (0, 2, 3, 3), (0, 2, 1, 3), (3, 3, 3, 1),
    (3, 3, 1, 1), (0, 3, 2, 0), (0, 2, 3, 4), (0, 1, 2, 0), (0, 2, 1, 4), (0, 0, 2, 3), (0, 0, 2, 4), (2, 0, 2, 0),
    (3, 1, 3, 1), (3, 0, 2, 0), (3, 1, 1, 1), (0, 3, 2, 3), (0, 3, 2, 4), (0, 3, 2, 1), (2, 3, 2, 0), (0, 1, 2, 1),
    (3, 3, 2, 0), (0, 1, 2, 3), (0, 1, 2, 4), (2, 1, 2, 0), (3, 1, 2, 0), (1, 1, 3, 1), (0, 2, 2, 3), (1, 1, 2, 1),
    (0, 2, 1, 0), (2, 2, 1, 0), (0, 2, 3, 1), (2, 2, 3, 0), (0, 2, 2, 4), (3, 0, 2, 1), (3, 2, 1, 0), (3, 2, 3, 0),
    (3, 3, 2, 1), (3, 1, 2, 1), (0, 2, 2, 0), (0, 2, 2, 1), (2, 2, 2, 0), (3, 2, 1, 1), (3, 2, 3, 1), (4, 0, 0, 0),
    (3, 2, 2, 0), (3, 2, 2, 1), (4, 1, 0, 0),
)


def place_tables():
    place = np.arange(TILE)
    source, s, u = place // SHARE, place % SHARE // 2, place % 2
    used = place < SPOTS
    tile_rows = np.zeros((8, NODES // TILE, TILE))
    for zh in range(4):
        for core in range(2):
            block = (source * 4 + zh) * 2 + core
            tile = (block * STRIPS + s) // (TILE // STRIP)
            tile_rows[zh * 2 + core] = used & (np.arange(NODES // TILE)[:, None] == tile)
    tile_cols = np.zeros((4, 8, TILE))
    for q in range(4):
        tile_cols[q] = used & (np.arange(8)[:, None] == (q - s) % 4 + 4 * u)
    before = place[:, None] < place[None, :]
    flat = [m.reshape(-1, TILE) for m in (tile_rows, tile_cols, before)]
    return np.concatenate(flat).astype(jnp.bfloat16)


def kernel(sparse, *refs):
    if sparse:
        (sim_ref, live_ref, marks_ref, tables_ref, out_ref, flag_ref, *refs) = refs
        (packed, out_share, in_share, stage, mark, order, table, table_smem, take, take_smem, copy_sem, degree_x, *refs) = refs
    else:
        sim_ref, live_ref, out_ref, *refs = refs
    (panel, weighted, expanded, degree_own, degree_in, total_own, total_core, total_x, total_z, *refs) = refs
    send_sem, recv_w, recv_core, recv_a, recv_small, recv_share = refs
    row, col = lax.axis_index("row"), lax.axis_index("col")
    x, zh, core = row // 8, (row // 2) % 4, row % 2
    zl, y = col // 4, col % 4

    def to_x(d):
        return ((x + d + 4) % 4 * 4 + zh) * 2 + core, col

    def to_z(d):
        return (x * 4 + (zh + d + 4) % 4) * 2 + core, col

    def to_y(d):
        return row, zl * 4 + (y + d + 4) % 4

    to_pair = (row, (1 - zl) * 4 + y)
    to_core = (row + 1 - 2 * core, col)

    def to_pair_y(d):
        return row, (1 - zl) * 4 + (y + d + 4) % 4


    barrier = pltpu.get_barrier_semaphore()
    partners = [to(d) for to in (to_x, to_y, to_z, to_pair_y) for d in (1, 2, 3)] + [to_pair, to_core]
    for device in partners:
        pl.semaphore_signal(barrier, 1, device_id=device, device_id_type=MESH)

    for s in range(ROWS // STRIP):
        tile_row = (row * (ROWS // STRIP) + s) // (TILE // STRIP)
        for t in range(COLS // TILE):
            kept = live_ref[t, tile_row].astype(jnp.float32)
            strip = sim_ref[s * STRIP : (s + 1) * STRIP, t * TILE : (t + 1) * TILE]
            panel[col, s * STRIP : (s + 1) * STRIP, t * TILE : (t + 1) * TILE] = (
                strip.astype(jnp.float32) * kept
            ).astype(jnp.bfloat16)
    adj = panel[col]
    ones = jnp.ones((8, COLS), jnp.bfloat16)
    sums = lax.dot_general(
        ones, adj, (((1,), (1,)), ((), ())), preferred_element_type=jnp.float32
    )
    degree_own[...] = jnp.zeros_like(degree_own)
    degree_own[:, :ROWS] = sums

    if sparse:
        marks = marks_ref[...].astype(jnp.float32).astype(jnp.bfloat16)
        tiles = NODES // TILE
        for zc in range(8):
            picked = jnp.dot(
                marks,
                tables_ref[zc * tiles : (zc + 1) * tiles, :],
                preferred_element_type=jnp.float32,
            )
            for q in range(4):
                first = 8 * tiles + q * 8
                columns = tables_ref[first : first + 8, :].astype(jnp.float32)[: COLS // TILE]
                mark[q * 8 + zc : q * 8 + zc + 1, :] = jnp.sum(
                    picked * columns, axis=0, keepdims=True
                )
        live = mark[...]
        before = jnp.dot(
            live.astype(jnp.bfloat16),
            tables_ref[8 * tiles + 32 :, :],
            preferred_element_type=jnp.float32,
        )
        order[...] = before + live
        most = jnp.max(jnp.max(before + live, axis=1, keepdims=True), axis=0, keepdims=True)
        degree_own[:, ROWS:] = jnp.broadcast_to(most, (8, 256 - ROWS))
        table[...] = jnp.where((live > 0) & (before < SLOTS), before, SLOTS).astype(jnp.int32)
        slot = lax.broadcasted_iota(jnp.int32, (32, TILE), 0).astype(jnp.float32)
        spot = lax.broadcasted_iota(jnp.int32, (32, TILE), 1)
        passed = jnp.where((order[pl.ds(row, 1), :] <= slot) & (spot < SPOTS), 1.0, 0.0)
        index = jnp.minimum(jnp.sum(passed, axis=1, keepdims=True), SPOTS - 1.0)
        take[...] = jnp.broadcast_to(index, (32, TILE)).astype(jnp.int32)
        table_copy = pltpu.make_async_copy(table, table_smem, copy_sem.at[0])
        take_copy = pltpu.make_async_copy(take, take_smem, copy_sem.at[1])
        table_copy.start()
        take_copy.start()
        out_share[...] = jnp.zeros_like(out_share)
        for q in range(4):
            for s in range(STRIPS):
                for u in (0, 1):
                    t = (q - s) % 4 + 4 * u
                    if t < COLS // TILE:
                        out_share[q, s * 2 + u] = adj[
                            s * STRIP : (s + 1) * STRIP, t * TILE : (t + 1) * TILE
                        ]
        stage[SLOTS] = jnp.zeros((STRIP, TILE), jnp.bfloat16)

    pl.semaphore_wait(barrier, len(partners))

    sends = []

    def send(src, dst, recv, device):
        copy = pltpu.make_async_remote_copy(
            src, dst, send_sem.at[len(sends)], recv, device_id=device, device_id_type=MESH
        )
        copy.start()
        sends.append(copy)

    def arrived(ref, recv):
        pltpu.make_async_remote_copy(
            ref, ref, send_sem.at[0], recv, device_id=to_core, device_id_type=MESH
        ).wait_recv()

    def a_ref(pair, dy, half):
        slot = (zl if pair == 0 else 1 - zl) * 4 + (y + dy + 4) % 4
        return panel.at[slot, pl.ds(half * PANEL_HALF, PANEL_HALF)]

    def a_send_pair(half):
        ref = a_ref(0, 0, half)
        send(ref, ref, recv_a.at[1, 0, half], to_pair)

    def a_send_y(pair, dy, half, step):
        ref = a_ref(pair, dy, half)
        send(ref, ref, recv_a.at[pair, (dy - step) % 4, half], to_y(step))

    def a_wait(pair, dy, half):
        arrived(a_ref(pair, dy, half), recv_a.at[pair, dy % 4, half])

    def w_row(dx, dz, which):
        return (((x + dx + 4) % 4) * 4 + (zh + dz + 4) % 4) * 2 + which

    def w_ref(dx, dz, piece):
        if sparse:
            start, size = SLOT_PARTS[piece]
            return packed.at[w_row(dx, dz, core), pl.ds(start, size)]
        start, size = ROW_PARTS[piece]
        first = pl.multiple_of(w_row(dx, dz, core) * ROWS + start, 16)
        return weighted.at[pl.ds(first, size)]

    def w_send(dx, dz, piece, axis, step):
        ref = w_ref(dx, dz, piece)
        nx, nz = (dx - step, dz) if axis == 0 else (dx, dz - step)
        send(
            ref,
            ref,
            recv_w.at[nx % 4, nz % 4, piece],
            to_x(step) if axis == 0 else to_z(step),
        )

    def w_wait(dx, dz, piece):
        arrived(w_ref(dx, dz, piece), recv_w.at[dx % 4, dz % 4, piece])

    def w_block(dx, dz, which):
        if sparse:
            return packed.at[w_row(dx, dz, which)]
        return weighted.at[pl.ds(pl.multiple_of(w_row(dx, dz, which) * ROWS, 16), ROWS)]

    def share(dx, dz):
        ref = w_block(dx, dz, core)
        send(ref, ref, recv_core.at[dx % 4, dz % 4], to_core)

    def shared(dx, dz):
        arrived(w_block(dx, dz, 1 - core), recv_core.at[dx % 4, dz % 4])

    for d in (2, 1, 3):
        send(degree_own, degree_in.at[8 - d], recv_small.at[24 - d], to_pair_y(d))
    for d in (2, 1, 3):
        send(degree_own, degree_in.at[4 - d], recv_small.at[20 - d], to_y(d))
    send(degree_own, degree_in.at[4], recv_small.at[20], to_pair)
    if sparse:
        for d in (2, 1, 3):
            there = (x + d) % 4
            send(out_share.at[there], in_share.at[pl.ds(x * SHARE, SHARE)], recv_share.at[4 - d], to_x(d))
    for half in (0, 1):
        a_send_pair(half)
    for half in (0, 1):
        a_send_y(0, 0, half, 1)
        a_send_y(0, 0, 1 - half, -1)

    lane = lax.broadcasted_iota(jnp.int32, (8, 256), 1)

    def join(a, b):
        return jnp.where(lane < ROWS, a + b, jnp.maximum(a, b))

    degree = degree_own[...]
    for d in (4, 1, 3, 2, 5, 7, 6):
        arrived(degree_in.at[d], recv_small.at[16 + d])
        degree = join(degree, degree_in[d])
    if sparse:
        flag_ref[...] = degree[:, TILE:]
        degree_x[0] = degree
        for d in (2, 1, 3):
            send(degree_x.at[0], degree_x.at[4 - d], recv_small.at[16 - d], to_x(d))
        in_share[pl.ds(x * SHARE, SHARE)] = out_share[x]
        table_copy.wait()
        take_copy.wait()
        for d in (0, 1, 3, 2):
            source = (x + d) % 4
            if d:
                arrived(in_share.at[pl.ds(source * SHARE, SHARE)], recv_share.at[d])
                arrived(degree_x.at[d], recv_small.at[12 + d])
            degree_column = jnp.transpose(degree_x[d])[:ROWS, 0:1]
            for s in range(STRIPS):
                column = degree_column[s * STRIP : (s + 1) * STRIP]
                for u in (0, 1):
                    place = source * SHARE + 2 * s + u
                    piece = in_share[place].astype(jnp.float32)
                    in_share[place] = (piece / column).astype(jnp.bfloat16)
        for k in range(SLOTS):
            packed[row, k] = in_share[jnp.clip(take_smem[k, 0], 0, SPOTS - 1)]
    else:
        degree_column = jnp.transpose(degree)[:ROWS, 0:1]
        scaled = (adj.astype(jnp.float32) / degree_column).astype(jnp.bfloat16)
        weighted[pl.ds(pl.multiple_of(row * ROWS, 16), ROWS), :] = scaled

    w_send(0, 0, TOP, 1, 1)
    w_send(0, 0, BOTTOM, 1, -1)
    w_send(0, 0, TOP, 0, 1)
    w_send(0, 0, BOTTOM, 0, -1)
    w_send(0, 0, EDGE, 0, 1)
    w_send(0, 0, EDGE, 0, -1)
    w_send(0, 0, BOTTOM, 1, 1)
    w_send(0, 0, TOP, 1, -1)
    w_send(0, 0, BOTTOM, 0, 1)
    w_send(0, 0, TOP, 0, -1)
    share(0, 0)

    late = []

    def edge_along_z(dx, piece):
        if late is None:
            w_send(dx, 0, piece, 1, 1)
            w_send(dx, 0, piece, 1, -1)
        else:
            late.append((dx, piece))

    def weighted_arrived(dx, dz, piece):
        nonlocal late
        w_wait(dx, dz, piece)
        if dz == 0 and piece > BOTTOM:
            if (dx, piece) in ((3, EDGE), (1, EDGE)):
                w_send(dx, 0, EDGE_TOP if dx == 3 else EDGE_BOTTOM, 0, dx - 2)
            edge_along_z(dx, piece)
        elif piece > BOTTOM:
            if dz == 3 and piece != EDGE_BOTTOM:
                w_send(dx, dz, EDGE_TOP, 1, 1)
            if dz == 1 and piece != EDGE_TOP:
                w_send(dx, dz, EDGE_BOTTOM, 1, -1)
        elif dx == 0:
            if (dz, piece) in ((3, TOP), (1, BOTTOM)):
                w_send(0, dz, piece, 1, dz - 2)
            w_send(0, dz, piece, 0, 1)
            w_send(0, dz, piece, 0, -1)
        elif (dx, piece) in ((3, TOP), (1, BOTTOM)):
            w_send(dx, dz, piece, 0, dx - 2)
        if (dx, dz, piece) == (0, 3, BOTTOM):
            held, late = late, None
            for item in held:
                edge_along_z(*item)

    def panel_arrived(pair, dy, half):
        a_wait(pair, dy, half)
        if (pair, dy) == (1, 0):
            a_send_y(1, 0, half, 1 - 2 * half)
        if (pair, dy) == (0, 2):
            a_send_y(1, 0, 1 - half, 1 - 2 * half)
        if (dy, half) in ((3, 0), (1, 1)):
            a_send_y(pair, dy, half, dy - 2)

    def unpack(dx, dz, which):
        xx, zz = (x + dx + 4) % 4, (zh + dz + 4) % 4
        block = w_row(dx, dz, which)
        stage[:SLOTS] = packed[block]

        @pl.loop(0, STRIPS)
        def _(s):
            t = (xx - s + 8) % 4
            for source in range(4):
                first = ((source * 4 + zz) * 2 + which) * ROWS + s * STRIP
                for u in (0, 1):
                    slot = table_smem[block, source * SHARE + 2 * s + u]
                    piece = stage[jnp.clip(slot, 0, SLOTS)]
                    weighted[t + 4 * u, pl.ds(pl.multiple_of(first, STRIP), STRIP)] = piece

    def multiply_pair(pair, first):
        for n in range(0, COLS // TILE, 2):
            width = min(2, COLS // TILE - n)
            left, right = [], []
            for source in range(4):
                group = source * 2 + pair
                depth = pl.ds(pl.multiple_of(group * COLS, 16), COLS)
                part = weighted[n, depth]
                if width == 2:
                    part = jnp.concatenate([part, weighted[n + 1, depth]], axis=1)
                left.append(panel[group])
                right.append(part)
            acc = jnp.dot(
                jnp.concatenate(left, axis=1),
                jnp.concatenate(right, axis=0),
                preferred_element_type=jnp.float32,
            )
            columns = slice(n * TILE, (n + width) * TILE)
            if first:
                expanded[:, columns] = acc
            else:
                expanded[:, columns] += acc

    def multiply(dx, first):
        xx = (x + dx) % 4

        for start in range(0, COLS, 256):
            size = min(256, COLS - start)
            acc = None
            for half in (0, 1):
                depth = pl.multiple_of((xx * 2 + half) * COLS, 16)
                part = jnp.dot(
                    panel[xx * 2 + half],
                    weighted[pl.ds(depth, COLS), start : start + size],
                    preferred_element_type=jnp.float32,
                )
                acc = part if acc is None else acc + part
            if first:
                expanded[:, start : start + size] = acc
            else:
                expanded[:, start : start + size] += acc

    edge_along_z(0, EDGE)
    for act, first, second, third in ORDER:
        if act == WEIGHTED:
            weighted_arrived(first, second, third)
        elif act == PANEL:
            panel_arrived(first, second, third)
        elif act == SHARED:
            share(first, second)
        elif act == UNPACK:
            if third:
                shared(first, second)
            if sparse:
                unpack(first, second, 1 - core if third else core)
        elif sparse:
            multiply_pair((zh // 2 + first) % 2, first == 0)
    if not sparse:
        for dx in range(4):
            multiply(dx, dx == 0)

    inflated = expanded[...] * expanded[...]
    part = jnp.sum(inflated, axis=0, keepdims=True)
    for t in range(COLS // TILE):
        total_own[0, t : t + 1, :] = part[:, t * TILE : (t + 1) * TILE]
    send(total_own.at[0], total_core, recv_small.at[4], to_core)
    arrived(total_core, recv_small.at[4])
    total_own[1] = total_own[0] + total_core[...]
    for d in (2, 1, 3):
        send(total_own.at[1], total_x.at[4 - d], recv_small.at[4 + 4 - d], to_x(d))
    part = total_own[1]
    for d in (1, 3, 2):
        arrived(total_x.at[d], recv_small.at[4 + d])
        part += total_x[d]
    total_own[2] = part
    for d in (2, 1, 3):
        send(total_own.at[2], total_z.at[4 - d], recv_small.at[8 + 4 - d], to_z(d))
    for d in (1, 3, 2):
        arrived(total_z.at[d], recv_small.at[8 + d])
        part += total_z[d]
    for t in range(COLS // TILE):
        columns = slice(t * TILE, (t + 1) * TILE)
        out_ref[:, columns] = NODES * inflated[:, columns] / part[t : t + 1, :]
    for copy in sends:
        copy.wait_send()


def call(sparse, *operands):
    vmem, sem = pltpu.VMEM, pltpu.SemaphoreType.DMA
    bf16, f32, i32 = jnp.bfloat16, jnp.float32, jnp.int32
    small, tile, table = (8, 256), (8, TILE), (32, TILE)
    flow = jax.ShapeDtypeStruct((ROWS, COLS), f32)
    in_vmem = pl.BlockSpec(memory_space=vmem)
    extra = []
    if sparse:
        extra = [
            vmem((ROW_DEVICES, SLOTS, STRIP, TILE), bf16),
            vmem((4, SHARE, STRIP, TILE), bf16),
            vmem((SPOTS, STRIP, TILE), bf16),
            vmem((SLOTS + 1, STRIP, TILE), bf16),
            vmem(table, f32),
            vmem(table, f32),
            vmem(table, i32),
            pltpu.SMEM(table, i32),
            vmem(table, i32),
            pltpu.SMEM(table, i32),
            sem((2,)),
            vmem((4, *small), f32),
        ]
    return pl.pallas_call(
        functools.partial(kernel, sparse),
        out_shape=[flow, jax.ShapeDtypeStruct(tile, f32)] if sparse else flow,
        in_specs=[in_vmem, pl.BlockSpec(memory_space=pltpu.SMEM)] + [in_vmem] * (len(operands) - 2),
        out_specs=[in_vmem, in_vmem] if sparse else in_vmem,
        scratch_shapes=[
            *extra,
            vmem((COL_DEVICES, ROWS, COLS), bf16),
            vmem((8, NODES, TILE) if sparse else (NODES, COLS), bf16),
            vmem((ROWS, COLS), f32),
            vmem(small, f32),
            vmem((8, *small), f32),
            vmem((3, *tile), f32),
            vmem(tile, f32),
            vmem((4, *tile), f32),
            vmem((4, *tile), f32),
            sem((SENDS,)),
            sem((4, 4, 5)),
            sem((4, 4)),
            sem((2, 4, 2)),
            sem((32,)),
            sem((4,)),
        ],
        compiler_params=pltpu.CompilerParams(
            collective_id=0 if sparse else 1,
            has_side_effects=True,
            vmem_limit_bytes=40 * 2**20,
        ),
        name="flow_of_packed" if sparse else "flow_of_whole",
    )(*operands)


def per_device(sim, live):
    marks = live.T
    flow, most = call(True, sim, marks, marks, jnp.asarray(place_tables()))
    return lax.cond(
        most[0, TILE - 1] <= SLOTS, lambda: flow, lambda: call(False, sim, marks)
    )


def solution(mesh):
    return jax.shard_map(
        per_device,
        mesh=mesh,
        in_specs=(P("row", "col"), P(None, "col")),
        out_specs=P("row", "col"),
        check_vma=False,
    )
```

```python
import functools

import jax
import jax.numpy as jnp
import numpy as np
from jax import lax
from jax.experimental import pallas as pl
from jax.experimental.pallas import tpu as pltpu
from jax.sharding import PartitionSpec as P

MESH = pl.DeviceIdType.MESH
TILE = 128
STRIP = 32
ROWS = 224
COLS = 896
ROW_DEVICES = 32
COL_DEVICES = 8
NODES = 7168
TOP, BOTTOM, EDGE, EDGE_TOP, EDGE_BOTTOM = 0, 1, 2, 3, 4


def parts_of(half, edge):
    return {
        TOP: (0, half),
        BOTTOM: (half, half),
        EDGE: (2 * half, 2 * edge),
        EDGE_TOP: (2 * half, edge),
        EDGE_BOTTOM: (2 * half + edge, edge),
    }


ROW_PARTS = parts_of(96, 16)
SLOTS = 22
SLOT_PARTS = parts_of(9, 2)
STRIPS = ROWS // STRIP
SHARE = 2 * STRIPS
SPOTS = 4 * SHARE
PANEL_HALF = ROWS // 2
SENDS = 128


WEIGHTED, PANEL, SHARED, UNPACK, MULTIPLY = range(5)
ORDER = (
    (1, 1, 0, 0), (1, 0, 3, 0), (1, 0, 1, 1), (1, 1, 0, 1), (1, 0, 3, 1), (1, 0, 1, 0), (3, 0, 0, 0), (3, 0, 0, 1),
    (0, 3, 0, 0), (0, 1, 0, 1), (0, 3, 0, 2), (0, 1, 0, 2), (0, 0, 3, 0), (0, 0, 1, 1), (0, 3, 0, 1), (2, 3, 0, 0),
    (0, 1, 0, 0), (2, 1, 0, 0), (3, 3, 0, 0), (3, 1, 0, 0), (1, 1, 3, 0), (1, 0, 2, 1), (0, 2, 0, 0), (0, 2, 0, 1),
    (0, 2, 0, 3), (0, 2, 0, 4), (2, 2, 0, 0), (3, 2, 0, 0), (3, 3, 0, 1), (3, 1, 0, 1), (0, 0, 3, 1), (0, 0, 1, 0),
    (0, 3, 3, 0), (0, 1, 3, 0), (3, 2, 0, 1), (0, 3, 1, 1), (0, 1, 1, 1), (1, 0, 2, 0), (1, 1, 1, 1), (0, 0, 2, 0),
    (0, 0, 2, 1), (0, 3, 3, 1), (0, 1, 3, 1), (0, 0, 3, 2), (2, 0, 3, 0), (0, 0, 1, 2), (2, 0, 1, 0), (3, 0, 3, 0),
    (3, 0, 1, 0), (0, 3, 1, 0), (0, 1, 1, 0), (0, 3, 3, 2), (2, 3, 3, 0), (0, 3, 1, 2), (2, 3, 1, 0), (3, 3, 3, 0),
    (3, 3, 1, 0), (3, 0, 3, 1), (1, 1, 2, 0), (0, 2, 3, 0), (0, 2, 1, 1), (0, 1, 3, 2), (2, 1, 3, 0), (1, 1, 1, 0),
    (0, 1, 1, 2), (2, 1, 1, 0), (3, 0, 1, 1), (3, 1, 3, 0), (3, 1, 1, 0), (0, 2, 3, 3), (0, 2, 1, 3), (3, 3, 3, 1),
    (3, 3, 1, 1), (0, 3, 2, 0), (0, 2, 3, 4), (0, 1, 2, 0), (0, 2, 1, 4), (0, 0, 2, 3), (0, 0, 2, 4), (2, 0, 2, 0),
    (3, 1, 3, 1), (3, 0, 2, 0), (3, 1, 1, 1), (0, 3, 2, 3), (0, 3, 2, 4), (0, 3, 2, 1), (2, 3, 2, 0), (0, 1, 2, 1),
    (3, 3, 2, 0), (0, 1, 2, 3), (0, 1, 2, 4), (2, 1, 2, 0), (3, 1, 2, 0), (1, 1, 3, 1), (0, 2, 2, 3), (1, 1, 2, 1),
    (0, 2, 1, 0), (2, 2, 1, 0), (0, 2, 3, 1), (2, 2, 3, 0), (0, 2, 2, 4), (3, 0, 2, 1), (3, 2, 1, 0), (3, 2, 3, 0),
    (3, 3, 2, 1), (3, 1, 2, 1), (0, 2, 2, 0), (0, 2, 2, 1), (2, 2, 2, 0), (3, 2, 1, 1), (3, 2, 3, 1), (4, 0, 0, 0),
    (3, 2, 2, 0), (3, 2, 2, 1), (4, 1, 0, 0),
)


def place_tables():
    place = np.arange(TILE)
    source, s, u = place // SHARE, place % SHARE // 2, place % 2
    used = place < SPOTS
    tile_rows = np.zeros((8, NODES // TILE, TILE))
    for zh in range(4):
        for core in range(2):
            block = (source * 4 + zh) * 2 + core
            tile = (block * STRIPS + s) // (TILE // STRIP)
            tile_rows[zh * 2 + core] = used & (np.arange(NODES // TILE)[:, None] == tile)
    tile_cols = np.zeros((4, 8, TILE))
    for q in range(4):
        tile_cols[q] = used & (np.arange(8)[:, None] == (q - s) % 4 + 4 * u)
    before = place[:, None] < place[None, :]
    flat = [m.reshape(-1, TILE) for m in (tile_rows, tile_cols, before)]
    return np.concatenate(flat).astype(jnp.bfloat16)


def kernel(sparse, *refs):
    if sparse:
        (sim_ref, live_ref, marks_ref, tables_ref, out_ref, flag_ref, *refs) = refs
        (packed, out_share, in_share, stage, mark, order, table, table_smem, take, take_smem, copy_sem, degree_x, degree_strip, *refs) = refs
    else:
        sim_ref, live_ref, out_ref, *refs = refs
    (panel, weighted, expanded, degree_own, degree_in, total_own, total_core, total_x, total_z, *refs) = refs
    send_sem, recv_w, recv_core, recv_a, recv_small, recv_share = refs
    row, col = lax.axis_index("row"), lax.axis_index("col")
    x, zh, core = row // 8, (row // 2) % 4, row % 2
    zl, y = col // 4, col % 4

    def to_x(d):
        return ((x + d + 4) % 4 * 4 + zh) * 2 + core, col

    def to_z(d):
        return (x * 4 + (zh + d + 4) % 4) * 2 + core, col

    def to_y(d):
        return row, zl * 4 + (y + d + 4) % 4

    to_pair = (row, (1 - zl) * 4 + y)
    to_core = (row + 1 - 2 * core, col)

    def to_pair_y(d):
        return row, (1 - zl) * 4 + (y + d + 4) % 4


    barrier = pltpu.get_barrier_semaphore()
    partners = [to(d) for to in (to_x, to_y, to_z, to_pair_y) for d in (1, 2, 3)] + [to_pair, to_core]
    for device in partners:
        pl.semaphore_signal(barrier, 1, device_id=device, device_id_type=MESH)

    for s in range(ROWS // STRIP):
        tile_row = (row * (ROWS // STRIP) + s) // (TILE // STRIP)
        for t in range(COLS // TILE):
            kept = live_ref[t, tile_row].astype(jnp.float32)
            strip = sim_ref[s * STRIP : (s + 1) * STRIP, t * TILE : (t + 1) * TILE]
            panel[col, s * STRIP : (s + 1) * STRIP, t * TILE : (t + 1) * TILE] = (
                strip.astype(jnp.float32) * kept
            ).astype(jnp.bfloat16)
    adj = panel[col]
    ones = jnp.ones((8, COLS), jnp.bfloat16)
    sums = lax.dot_general(
        ones, adj, (((1,), (1,)), ((), ())), preferred_element_type=jnp.float32
    )
    degree_own[...] = jnp.zeros_like(degree_own)
    degree_own[:, :ROWS] = sums

    if sparse:
        marks = marks_ref[...].astype(jnp.float32).astype(jnp.bfloat16)
        tiles = NODES // TILE
        for zc in range(8):
            picked = jnp.dot(
                marks,
                tables_ref[zc * tiles : (zc + 1) * tiles, :],
                preferred_element_type=jnp.float32,
            )
            for q in range(4):
                first = 8 * tiles + q * 8
                columns = tables_ref[first : first + 8, :].astype(jnp.float32)[: COLS // TILE]
                mark[q * 8 + zc : q * 8 + zc + 1, :] = jnp.sum(
                    picked * columns, axis=0, keepdims=True
                )
        live = mark[...]
        before = jnp.dot(
            live.astype(jnp.bfloat16),
            tables_ref[8 * tiles + 32 :, :],
            preferred_element_type=jnp.float32,
        )
        order[...] = before + live
        most = jnp.max(jnp.max(before + live, axis=1, keepdims=True), axis=0, keepdims=True)
        degree_own[:, ROWS:] = jnp.broadcast_to(most, (8, 256 - ROWS))
        table[...] = jnp.where((live > 0) & (before < SLOTS), before, SLOTS).astype(jnp.int32)
        slot = lax.broadcasted_iota(jnp.int32, (32, TILE), 0).astype(jnp.float32)
        spot = lax.broadcasted_iota(jnp.int32, (32, TILE), 1)
        passed = jnp.where((order[pl.ds(row, 1), :] <= slot) & (spot < SPOTS), 1.0, 0.0)
        index = jnp.minimum(jnp.sum(passed, axis=1, keepdims=True), SPOTS - 1.0)
        take[...] = jnp.broadcast_to(index, (32, TILE)).astype(jnp.int32)
        table_copy = pltpu.make_async_copy(table, table_smem, copy_sem.at[0])
        take_copy = pltpu.make_async_copy(take, take_smem, copy_sem.at[1])
        table_copy.start()
        take_copy.start()
        out_share[...] = jnp.zeros_like(out_share)
        for q in range(4):
            for s in range(STRIPS):
                for u in (0, 1):
                    t = (q - s) % 4 + 4 * u
                    if t < COLS // TILE:
                        out_share[q, s * 2 + u] = adj[
                            s * STRIP : (s + 1) * STRIP, t * TILE : (t + 1) * TILE
                        ]
        stage[SLOTS] = jnp.zeros((STRIP, TILE), jnp.bfloat16)

    pl.semaphore_wait(barrier, len(partners))

    sends = []

    def send(src, dst, recv, device):
        copy = pltpu.make_async_remote_copy(
            src, dst, send_sem.at[len(sends)], recv, device_id=device, device_id_type=MESH
        )
        copy.start()
        sends.append(copy)

    def arrived(ref, recv):
        pltpu.make_async_remote_copy(
            ref, ref, send_sem.at[0], recv, device_id=to_core, device_id_type=MESH
        ).wait_recv()

    def a_ref(pair, dy, half):
        slot = (zl if pair == 0 else 1 - zl) * 4 + (y + dy + 4) % 4
        return panel.at[slot, pl.ds(half * PANEL_HALF, PANEL_HALF)]

    def a_send_pair(half):
        ref = a_ref(0, 0, half)
        send(ref, ref, recv_a.at[1, 0, half], to_pair)

    def a_send_y(pair, dy, half, step):
        ref = a_ref(pair, dy, half)
        send(ref, ref, recv_a.at[pair, (dy - step) % 4, half], to_y(step))

    def a_wait(pair, dy, half):
        arrived(a_ref(pair, dy, half), recv_a.at[pair, dy % 4, half])

    def w_row(dx, dz, which):
        return (((x + dx + 4) % 4) * 4 + (zh + dz + 4) % 4) * 2 + which

    def w_ref(dx, dz, piece):
        if sparse:
            start, size = SLOT_PARTS[piece]
            return packed.at[w_row(dx, dz, core), pl.ds(start, size)]
        start, size = ROW_PARTS[piece]
        first = pl.multiple_of(w_row(dx, dz, core) * ROWS + start, 16)
        return weighted.at[pl.ds(first, size)]

    def w_send(dx, dz, piece, axis, step):
        ref = w_ref(dx, dz, piece)
        nx, nz = (dx - step, dz) if axis == 0 else (dx, dz - step)
        send(
            ref,
            ref,
            recv_w.at[nx % 4, nz % 4, piece],
            to_x(step) if axis == 0 else to_z(step),
        )

    def w_wait(dx, dz, piece):
        arrived(w_ref(dx, dz, piece), recv_w.at[dx % 4, dz % 4, piece])

    def w_block(dx, dz, which):
        if sparse:
            return packed.at[w_row(dx, dz, which)]
        return weighted.at[pl.ds(pl.multiple_of(w_row(dx, dz, which) * ROWS, 16), ROWS)]

    def share(dx, dz):
        ref = w_block(dx, dz, core)
        send(ref, ref, recv_core.at[dx % 4, dz % 4], to_core)

    def shared(dx, dz):
        arrived(w_block(dx, dz, 1 - core), recv_core.at[dx % 4, dz % 4])

    for d in (2, 1, 3):
        send(degree_own, degree_in.at[8 - d], recv_small.at[24 - d], to_pair_y(d))
    for d in (2, 1, 3):
        send(degree_own, degree_in.at[4 - d], recv_small.at[20 - d], to_y(d))
    send(degree_own, degree_in.at[4], recv_small.at[20], to_pair)
    if sparse:
        for d in (2, 1, 3):
            there = (x + d) % 4
            send(out_share.at[there], in_share.at[pl.ds(x * SHARE, SHARE)], recv_share.at[4 - d], to_x(d))
    for half in (0, 1):
        a_send_pair(half)
    for half in (0, 1):
        a_send_y(0, 0, half, 1)
        a_send_y(0, 0, 1 - half, -1)

    lane = lax.broadcasted_iota(jnp.int32, (8, 256), 1)

    def join(a, b):
        return jnp.where(lane < ROWS, a + b, jnp.maximum(a, b))

    degree = degree_own[...]
    for d in (4, 1, 3, 2, 5, 7, 6):
        arrived(degree_in.at[d], recv_small.at[16 + d])
        degree = join(degree, degree_in[d])
    if sparse:
        flag_ref[...] = degree[:, TILE:]
        degree_x[0] = degree
        for d in (2, 1, 3):
            send(degree_x.at[0], degree_x.at[4 - d], recv_small.at[16 - d], to_x(d))
        in_share[pl.ds(x * SHARE, SHARE)] = out_share[x]
        table_copy.wait()
        take_copy.wait()
        for d in (1, 3, 2):
            arrived(degree_x.at[d], recv_small.at[12 + d])
        ring = lax.broadcasted_iota(jnp.int32, (8, 256), 0)
        columns = degree
        for d in (1, 2, 3):
            columns = jnp.where(ring == d, degree_x[d], columns)
        columns = jnp.transpose(columns)
        for d in range(4):
            for s in range(STRIPS):
                column = columns[s * STRIP : (s + 1) * STRIP, d : d + 1]
                degree_strip[(x + d) % 4 * STRIPS + s] = jnp.broadcast_to(column, (STRIP, TILE))
        for d in (1, 3, 2):
            arrived(in_share.at[pl.ds((x + d) % 4 * SHARE, SHARE)], recv_share.at[d])
        for k in range(SLOTS):
            place = jnp.clip(take_smem[k, 0], 0, SPOTS - 1)
            piece = in_share[place].astype(jnp.float32) / degree_strip[place // 2]
            packed[row, k] = piece.astype(jnp.bfloat16)
    else:
        degree_column = jnp.transpose(degree)[:ROWS, 0:1]
        scaled = (adj.astype(jnp.float32) / degree_column).astype(jnp.bfloat16)
        weighted[pl.ds(pl.multiple_of(row * ROWS, 16), ROWS), :] = scaled

    w_send(0, 0, TOP, 1, 1)
    w_send(0, 0, BOTTOM, 1, -1)
    w_send(0, 0, TOP, 0, 1)
    w_send(0, 0, BOTTOM, 0, -1)
    w_send(0, 0, EDGE, 0, 1)
    w_send(0, 0, EDGE, 0, -1)
    w_send(0, 0, BOTTOM, 1, 1)
    w_send(0, 0, TOP, 1, -1)
    w_send(0, 0, BOTTOM, 0, 1)
    w_send(0, 0, TOP, 0, -1)
    share(0, 0)

    late = []

    def edge_along_z(dx, piece):
        if late is None:
            w_send(dx, 0, piece, 1, 1)
            w_send(dx, 0, piece, 1, -1)
        else:
            late.append((dx, piece))

    def weighted_arrived(dx, dz, piece):
        nonlocal late
        w_wait(dx, dz, piece)
        if dz == 0 and piece > BOTTOM:
            if (dx, piece) in ((3, EDGE), (1, EDGE)):
                w_send(dx, 0, EDGE_TOP if dx == 3 else EDGE_BOTTOM, 0, dx - 2)
            edge_along_z(dx, piece)
        elif piece > BOTTOM:
            if dz == 3 and piece != EDGE_BOTTOM:
                w_send(dx, dz, EDGE_TOP, 1, 1)
            if dz == 1 and piece != EDGE_TOP:
                w_send(dx, dz, EDGE_BOTTOM, 1, -1)
        elif dx == 0:
            if (dz, piece) in ((3, TOP), (1, BOTTOM)):
                w_send(0, dz, piece, 1, dz - 2)
            w_send(0, dz, piece, 0, 1)
            w_send(0, dz, piece, 0, -1)
        elif (dx, piece) in ((3, TOP), (1, BOTTOM)):
            w_send(dx, dz, piece, 0, dx - 2)
        if (dx, dz, piece) == (0, 3, BOTTOM):
            held, late = late, None
            for item in held:
                edge_along_z(*item)

    def panel_arrived(pair, dy, half):
        a_wait(pair, dy, half)
        if (pair, dy) == (1, 0):
            a_send_y(1, 0, half, 1 - 2 * half)
        if (pair, dy) == (0, 2):
            a_send_y(1, 0, 1 - half, 1 - 2 * half)
        if (dy, half) in ((3, 0), (1, 1)):
            a_send_y(pair, dy, half, dy - 2)

    def unpack(dx, dz, which):
        xx, zz = (x + dx + 4) % 4, (zh + dz + 4) % 4
        block = w_row(dx, dz, which)
        stage[:SLOTS] = packed[block]

        @pl.loop(0, STRIPS)
        def _(s):
            t = (xx - s + 8) % 4
            for source in range(4):
                first = ((source * 4 + zz) * 2 + which) * ROWS + s * STRIP
                for u in (0, 1):
                    slot = table_smem[block, source * SHARE + 2 * s + u]
                    piece = stage[jnp.clip(slot, 0, SLOTS)]
                    weighted[t + 4 * u, pl.ds(pl.multiple_of(first, STRIP), STRIP)] = piece

    def multiply_pair(pair, first):
        for n in range(0, COLS // TILE, 2):
            width = min(2, COLS // TILE - n)
            left, right = [], []
            for source in range(4):
                group = source * 2 + pair
                depth = pl.ds(pl.multiple_of(group * COLS, 16), COLS)
                part = weighted[n, depth]
                if width == 2:
                    part = jnp.concatenate([part, weighted[n + 1, depth]], axis=1)
                left.append(panel[group])
                right.append(part)
            acc = jnp.dot(
                jnp.concatenate(left, axis=1),
                jnp.concatenate(right, axis=0),
                preferred_element_type=jnp.float32,
            )
            columns = slice(n * TILE, (n + width) * TILE)
            if first:
                expanded[:, columns] = acc
            else:
                acc += expanded[:, columns]
                expanded[:, columns] = acc * acc

    def multiply(dx, first):
        xx = (x + dx) % 4

        for start in range(0, COLS, 256):
            size = min(256, COLS - start)
            acc = None
            for half in (0, 1):
                depth = pl.multiple_of((xx * 2 + half) * COLS, 16)
                part = jnp.dot(
                    panel[xx * 2 + half],
                    weighted[pl.ds(depth, COLS), start : start + size],
                    preferred_element_type=jnp.float32,
                )
                acc = part if acc is None else acc + part
            if first:
                expanded[:, start : start + size] = acc
            else:
                expanded[:, start : start + size] += acc

    edge_along_z(0, EDGE)
    for act, first, second, third in ORDER:
        if act == WEIGHTED:
            weighted_arrived(first, second, third)
        elif act == PANEL:
            panel_arrived(first, second, third)
        elif act == SHARED:
            share(first, second)
        elif act == UNPACK:
            if third:
                shared(first, second)
            if sparse:
                unpack(first, second, 1 - core if third else core)
        elif sparse:
            multiply_pair((zh // 2 + first) % 2, first == 0)
    if not sparse:
        for dx in range(4):
            multiply(dx, dx == 0)

    inflated = expanded[...] if sparse else expanded[...] * expanded[...]
    part = jnp.sum(inflated, axis=0, keepdims=True)
    for t in range(COLS // TILE):
        total_own[0, t : t + 1, :] = part[:, t * TILE : (t + 1) * TILE]
    send(total_own.at[0], total_core, recv_small.at[4], to_core)
    arrived(total_core, recv_small.at[4])
    total_own[1] = total_own[0] + total_core[...]
    for d in (2, 1, 3):
        send(total_own.at[1], total_x.at[4 - d], recv_small.at[4 + 4 - d], to_x(d))
    part = total_own[1]
    for d in (1, 3, 2):
        arrived(total_x.at[d], recv_small.at[4 + d])
        part += total_x[d]
    total_own[2] = part
    for d in (2, 1, 3):
        send(total_own.at[2], total_z.at[4 - d], recv_small.at[8 + 4 - d], to_z(d))
    for d in (1, 3, 2):
        arrived(total_z.at[d], recv_small.at[8 + d])
        part += total_z[d]
    for t in range(COLS // TILE):
        columns = slice(t * TILE, (t + 1) * TILE)
        out_ref[:, columns] = NODES * inflated[:, columns] / part[t : t + 1, :]
    for copy in sends:
        copy.wait_send()


def call(sparse, *operands):
    vmem, sem = pltpu.VMEM, pltpu.SemaphoreType.DMA
    bf16, f32, i32 = jnp.bfloat16, jnp.float32, jnp.int32
    small, tile, table = (8, 256), (8, TILE), (32, TILE)
    flow = jax.ShapeDtypeStruct((ROWS, COLS), f32)
    in_vmem = pl.BlockSpec(memory_space=vmem)
    extra = []
    if sparse:
        extra = [
            vmem((ROW_DEVICES, SLOTS, STRIP, TILE), bf16),
            vmem((4, SHARE, STRIP, TILE), bf16),
            vmem((SPOTS, STRIP, TILE), bf16),
            vmem((SLOTS + 1, STRIP, TILE), bf16),
            vmem(table, f32),
            vmem(table, f32),
            vmem(table, i32),
            pltpu.SMEM(table, i32),
            vmem(table, i32),
            pltpu.SMEM(table, i32),
            sem((2,)),
            vmem((4, *small), f32),
            vmem((4 * STRIPS, STRIP, TILE), f32),
        ]
    return pl.pallas_call(
        functools.partial(kernel, sparse),
        out_shape=[flow, jax.ShapeDtypeStruct(tile, f32)] if sparse else flow,
        in_specs=[in_vmem, pl.BlockSpec(memory_space=pltpu.SMEM)] + [in_vmem] * (len(operands) - 2),
        out_specs=[in_vmem, in_vmem] if sparse else in_vmem,
        scratch_shapes=[
            *extra,
            vmem((COL_DEVICES, ROWS, COLS), bf16),
            vmem((8, NODES, TILE) if sparse else (NODES, COLS), bf16),
            vmem((ROWS, COLS), f32),
            vmem(small, f32),
            vmem((8, *small), f32),
            vmem((3, *tile), f32),
            vmem(tile, f32),
            vmem((4, *tile), f32),
            vmem((4, *tile), f32),
            sem((SENDS,)),
            sem((4, 4, 5)),
            sem((4, 4)),
            sem((2, 4, 2)),
            sem((32,)),
            sem((4,)),
        ],
        compiler_params=pltpu.CompilerParams(
            collective_id=0 if sparse else 1,
            has_side_effects=True,
            vmem_limit_bytes=40 * 2**20,
        ),
        name="flow_of_packed" if sparse else "flow_of_whole",
    )(*operands)


def per_device(sim, live):
    marks = live.T
    flow, most = call(True, sim, marks, marks, jnp.asarray(place_tables()))
    return lax.cond(
        most[0, TILE - 1] <= SLOTS, lambda: flow, lambda: call(False, sim, marks)
    )


def solution(mesh):
    return jax.shard_map(
        per_device,
        mesh=mesh,
        in_specs=(P("row", "col"), P(None, "col")),
        out_specs=P("row", "col"),
        check_vma=False,
    )
```
